512 devices in a mesh: dp: 4 (over y_hi), expert: 128 (over y_lo, x, z, core).
Axes of the slice: x: 4, y: 8 (y_hi: 4, y_lo: 2; y = y_hi * 2 + y_lo), z: 8, core: 2. Of those that a mesh axis runs over, the one named last changes fastest.
Arguments:
- tokens: bfloat16 [512, 196, 768], P(('dp', 'expert')), may hold values from -100 to 100
- router: bfloat16 [768, 128], replicated
- up_weight: bfloat16 [128, 768, 3072], P('expert', None, 'dp'), may hold values from -0.21875 to 0.21875
- down_weight: bfloat16 [128, 3072, 768], P('expert', 'dp'), may hold values from -0.109375 to 0.109375
- cotangent: bfloat16 [512, 196, 768], P(('dp', 'expert')), may hold values from -6 to 6
Outputs:
- grad_tokens: bfloat16 [512, 196, 768], P(('dp', 'expert'))
- grad_router: float32 [768, 128], replicated
- grad_down: bfloat16 [128, 3072, 768], P('expert', 'dp')
The draws below stay inside these ranges and needn't reach their ends.
All inputs are finite; a program needn't handle non-finite values.
Results may differ from the reference program's by a relative error of at most 0.008.
Values may be sent and summed in bfloat16 or wider, within the bound.
No kernel may reach another device: no remote copies, remote signals or barrier semaphores. Data moves between devices by JAX's collectives and lax.ppermute only.
A program may use at most 64 MiB of HBM per device.

```python
import math
import jax
import jax.numpy as jnp
from jax import lax

D = 768
FF = 3072
M = 196
EXPERTS = 128
IMAGES = 512


def draw_tokens(key, part):
    key = jax.random.fold_in(key, 11)
    first_key = jax.random.fold_in(key, 0)
    values = jnp.clip(jax.random.normal(first_key, (IMAGES, M, D), jnp.float32), -6.0, 6.0)
    return values.astype(jnp.bfloat16)


def draw_router(key, part):
    key = jax.random.fold_in(key, 23)
    first_key = jax.random.fold_in(key, 0)
    spread = 3.0 / math.sqrt(D)
    values = jnp.clip(jax.random.normal(first_key, (D, EXPERTS), jnp.float32) * spread, -6.0 * spread, 6.0 * spread)
    return values.astype(jnp.bfloat16)


def shard_levels(stream_key, extent, shards, low, top_value):
    level = 1.0
    for dim, parts in shards:
        draws = jax.random.uniform(jax.random.fold_in(jax.random.fold_in(stream_key, 6), dim), (parts,), jnp.float32, low / len(shards), top_value / len(shards))
        level = level * jnp.repeat(jnp.exp(draws), extent[dim] // parts).reshape((-1,) + (1,) * (len(extent) - 1 - dim))
    return level


def bell_draw(stream_key, extent, width, limit, shards=(), kind=jnp.bfloat16):
    result = width * jax.random.normal(stream_key, extent, jnp.float32)
    if shards:
        result = result * shard_levels(stream_key, extent, shards, -0.22, 0.18)
    return jnp.clip(result, -limit, limit).astype(kind)


def setup_inputs(seed: int = 0) -> dict:
    keys = jax.random.split(jax.random.key(seed), 6)
    return {
        "tokens": draw_tokens(jax.random.fold_in(keys[5], 71), 0),
        "router": draw_router(jax.random.fold_in(keys[5], 71), 0),
        "up_weight": bell_draw(keys[2], (EXPERTS, D, FF), D ** -0.5, 0.21875, ((0, 128), (2, 4))),
        "down_weight": bell_draw(keys[3], (EXPERTS, FF, D), FF ** -0.5, 0.109375, ((0, 128), (1, 4))),
        "cotangent": bell_draw(keys[4], (IMAGES, M, D), 1.0, 6.0, ((0, 512),)),
    }


GELU_SCALE = math.sqrt(2.0 / math.pi)
GELU_CUBIC = 0.044715

def gelu_tanh(values):
    return 0.5 * values * (1.0 + jnp.tanh(GELU_SCALE * (values + GELU_CUBIC * values * values * values)))

def gelu_slope(values):
    inner = jnp.tanh(GELU_SCALE * (values + GELU_CUBIC * values * values * values))
    return 0.5 * (1.0 + inner) + 0.5 * values * (1.0 - inner * inner) * GELU_SCALE * (1.0 + 3.0 * GELU_CUBIC * values * values)

def per_expert(packed):
    slot_rows, slot_grad_rows, weight_up, weight_down = packed
    hidden_pre = jnp.dot(slot_rows, weight_up, preferred_element_type=jnp.float32)
    activation = gelu_tanh(hidden_pre).astype(jnp.bfloat16)
    outputs = jnp.dot(activation, weight_down, preferred_element_type=jnp.float32).astype(jnp.bfloat16)
    upstream = jnp.dot(slot_grad_rows, weight_down.T, preferred_element_type=jnp.float32)
    hidden_grad = (upstream * gelu_slope(hidden_pre)).astype(jnp.bfloat16)
    down_grad = jnp.dot(activation.T, slot_grad_rows, preferred_element_type=jnp.float32).astype(jnp.bfloat16)
    input_grad = jnp.dot(hidden_grad, weight_up.T, preferred_element_type=jnp.float32).astype(jnp.bfloat16)
    return (outputs, down_grad, input_grad)

def reference(tokens, router, up_weight, down_weight, cotangent):
    tokens_wide = tokens.astype(jnp.float32)
    router_wide = router.astype(jnp.float32)
    cotangent_wide = cotangent.astype(jnp.float32)
    logits = jnp.einsum('bmd,ds->bms', tokens_wide, router_wide)
    dispatch = jax.nn.softmax(logits, axis=1)
    combine = jax.nn.softmax(logits, axis=2)
    dispatch_low = dispatch.astype(jnp.bfloat16)
    combine_low = combine.astype(jnp.bfloat16)
    slot_inputs = jnp.einsum('bms,bmd->bsd', dispatch_low.astype(jnp.float32), tokens_wide).astype(jnp.bfloat16)
    slot_cotangent = jnp.einsum('bms,bmd->bsd', combine_low.astype(jnp.float32), cotangent_wide).astype(jnp.bfloat16)
    outputs, grad_down, input_rows = lax.map(per_expert, (jnp.transpose(slot_inputs, (1, 0, 2)), jnp.transpose(slot_cotangent, (1, 0, 2)), up_weight, down_weight))
    slot_outputs = jnp.transpose(outputs, (1, 0, 2))
    input_grads = jnp.transpose(input_rows, (1, 0, 2))
    combine_grad = jnp.einsum('bmd,bsd->bms', cotangent_wide, slot_outputs.astype(jnp.float32))
    dispatch_grad = jnp.einsum('bmd,bsd->bms', tokens_wide, input_grads.astype(jnp.float32))
    logit_grad = combine * (combine_grad - lax.optimization_barrier(jnp.sum(combine * combine_grad, axis=2, keepdims=True)))
    logit_grad = logit_grad + dispatch * (dispatch_grad - lax.optimization_barrier(jnp.sum(dispatch * dispatch_grad, axis=1, keepdims=True)))
    logit_low = logit_grad.astype(jnp.bfloat16).astype(jnp.float32)
    grad_tokens = jnp.einsum('bms,bsd->bmd', dispatch_low.astype(jnp.float32), input_grads.astype(jnp.float32))
    grad_tokens = grad_tokens + jnp.einsum('bms,ds->bmd', logit_low, router_wide)
    grad_router = jnp.einsum('bmd,bms->ds', tokens_wide, logit_low)
    return (grad_tokens.astype(jnp.bfloat16), grad_router, grad_down)
```

```python
import math

import jax
import jax.numpy as jnp
from jax import lax
from jax.sharding import PartitionSpec as P

GELU_SCALE = math.sqrt(2.0 / math.pi)
GELU_CUBIC = 0.044715
LOW = jnp.bfloat16
WIDE = jnp.float32


def gelu_parts(values):
    squared = values * values
    inner = jnp.tanh(GELU_SCALE * (values + GELU_CUBIC * squared * values))
    activation = 0.5 * values * (1.0 + inner)
    slope = 0.5 * (1.0 + inner) + 0.5 * values * (1.0 - inner * inner) * GELU_SCALE * (
        1.0 + 3.0 * GELU_CUBIC * squared
    )
    return activation, slope


def wide_einsum(spec, left, right):
    return jnp.einsum(spec, left, right, preferred_element_type=WIDE)


def expert_rows(rows, up, down):
    hidden_pre = wide_einsum("rd,df->rf", rows[0], up)
    activation, slope = gelu_parts(hidden_pre)
    activation = activation.astype(LOW)
    upstream = wide_einsum("rd,fd->rf", rows[1], down)
    hidden_grad = (upstream * slope).astype(LOW)
    outputs = wide_einsum("rf,fd->rd", activation, down)
    input_grads = wide_einsum("rf,df->rd", hidden_grad, up)
    return outputs, input_grads, activation


def shards(tokens, router, up_weight, down_weight, cotangent):
    tokens, cotangent = tokens[0], cotangent[0]
    up, down = up_weight[0], down_weight[0]
    dp = lax.axis_size("dp")
    here = lax.axis_index("dp")
    to_right = [(i, (i + 1) % dp) for i in range(dp)]
    to_left = [(i, (i - 1) % dp) for i in range(dp)]

    logits = wide_einsum("md,ds->ms", tokens, router)
    dispatch = jax.nn.softmax(logits, axis=0)
    combine = jax.nn.softmax(logits, axis=1)
    dispatch_low = dispatch.astype(LOW)
    combine_low = combine.astype(LOW)
    slot_inputs = wide_einsum("ms,md->sd", dispatch_low, tokens).astype(LOW)
    slot_cotangent = wide_einsum("ms,md->sd", combine_low, cotangent).astype(LOW)

    sent = jnp.stack([slot_inputs, slot_cotangent], axis=1)
    own_slots = lax.all_to_all(sent, "expert", split_axis=0, concat_axis=0, tiled=True)
    own_slots = jnp.swapaxes(own_slots, 0, 1)
    blocks = lax.all_gather(own_slots, "dp", axis=0)

    def block_of(offset):
        return lax.dynamic_index_in_dim(blocks, (here + offset) % dp, 0, keepdims=False)

    far_rows, right_rows, left_rows, own_rows = (block_of(k) for k in (2, 1, 3, 0))
    far_out, far_in, far_act = expert_rows(far_rows, up, down)
    from_left_far = lax.ppermute(far_out.astype(LOW), "dp", to_right)
    from_right_far = lax.ppermute(far_in.astype(LOW), "dp", to_left)
    right_out, right_in, right_act = expert_rows(right_rows, up, down)
    left_out, left_in, left_act = expert_rows(left_rows, up, down)
    own_out, own_in, own_act = expert_rows(own_rows, up, down)
    from_left = lax.ppermute(
        jnp.stack([(right_out + from_left_far.astype(WIDE)).astype(LOW), right_in.astype(LOW)]),
        "dp",
        to_right,
    )
    from_right = lax.ppermute(
        jnp.stack([left_out.astype(LOW), (left_in + from_right_far.astype(WIDE)).astype(LOW)]),
        "dp",
        to_left,
    )
    all_act = jnp.concatenate([far_act, right_act, left_act, own_act])
    all_grad = jnp.concatenate([far_rows[1], right_rows[1], left_rows[1], own_rows[1]])
    grad_down = wide_einsum("rf,rd->fd", all_act, all_grad).astype(LOW)
    summed = (
        jnp.stack([own_out, own_in]) + from_left.astype(WIDE) + from_right.astype(WIDE)
    ).astype(LOW)

    back = lax.all_to_all(
        jnp.swapaxes(summed, 0, 1), "expert", split_axis=0, concat_axis=0, tiled=True
    )
    slot_outputs, input_grads = back[:, 0], back[:, 1]

    combine_grad = wide_einsum("md,sd->ms", cotangent, slot_outputs)
    dispatch_grad = wide_einsum("md,sd->ms", tokens, input_grads)
    logit_grad = combine * (combine_grad - jnp.sum(combine * combine_grad, axis=1, keepdims=True))
    logit_grad = logit_grad + dispatch * (
        dispatch_grad - jnp.sum(dispatch * dispatch_grad, axis=0, keepdims=True)
    )
    logit_low = logit_grad.astype(LOW)

    router_term = wide_einsum("ms,md->sd", logit_low, tokens)
    by_slot = lax.all_to_all(router_term, "expert", split_axis=0, concat_axis=0, tiled=True)
    slot_sum = lax.psum(jnp.sum(by_slot, axis=0).reshape(6, 128), "dp").reshape(1, -1)
    everywhere = lax.all_to_all(
        jnp.broadcast_to(slot_sum, router_term.shape), "expert", split_axis=0, concat_axis=0, tiled=True
    )
    grad_router = everywhere.T

    grad_tokens = wide_einsum("ms,sd->md", dispatch_low, input_grads)
    grad_tokens = grad_tokens + wide_einsum("ms,ds->md", logit_low, router)
    return (grad_tokens.astype(LOW)[None], grad_router, grad_down[None])


def solution(mesh):
    placed = (
        P(("dp", "expert"), None, None),
        P(),
        P("expert", None, "dp"),
        P("expert", "dp", None),
        P(("dp", "expert"), None, None),
    )
    return jax.shard_map(
        shards,
        mesh=mesh,
        in_specs=placed,
        out_specs=(P(("dp", "expert"), None, None), P(), P("expert", "dp", None)),
        check_vma=False,
    )
```

```python
import functools
import math

import jax
import jax.numpy as jnp
from jax import lax
from jax.experimental import pallas as pl
from jax.experimental.pallas import tpu as pltpu
from jax.sharding import Mesh
from jax.sharding import PartitionSpec as P

GELU_SCALE = math.sqrt(2.0 / math.pi)
GELU_CUBIC = 0.044715
LOW = jnp.bfloat16
WIDE = jnp.float32
EXPERT_SPLIT = {"yl": 2, "x": 4, "z": 8, "core": 2}
EXPERT = tuple(EXPERT_SPLIT)
EVERY = ("dp",) + EXPERT
NEAR = ("yl", "x", "core")
REST = ("dp", "z")
VMEM_BYTES = 48 * 2**20


def wide_einsum(spec, left, right):
    return jnp.einsum(spec, left, right, preferred_element_type=WIDE)


def wide_dot(left, right, left_dim, right_dim):
    return lax.dot_general(
        left, right, (((left_dim,), (right_dim,)), ((), ())), preferred_element_type=WIDE
    )


def in_vmem(count):
    return [pl.BlockSpec(memory_space=pltpu.VMEM)] * count


def cost(flops, bytes_accessed):
    return pl.CostEstimate(flops=flops, bytes_accessed=bytes_accessed, transcendentals=0)


def expert_kernel(rows_ref, grads_ref, up_ref, down_ref, out_ref, in_ref, act_ref):
    up, down = up_ref[...], down_ref[...]
    hidden_pre = wide_dot(rows_ref[...], up, 1, 0)
    squared = hidden_pre * hidden_pre
    inner = jnp.tanh(GELU_SCALE * (hidden_pre + GELU_CUBIC * squared * hidden_pre))
    half = 0.5 * (1.0 + inner)
    activation = (hidden_pre * half).astype(LOW)
    act_ref[...] = activation
    out_ref[...] = wide_dot(activation, down, 1, 0).astype(out_ref.dtype)
    slope = half + 0.5 * hidden_pre * (1.0 - inner * inner) * (
        GELU_SCALE + 3.0 * GELU_SCALE * GELU_CUBIC * squared
    )
    upstream = wide_dot(grads_ref[...], down, 1, 1)
    hidden_grad = (upstream * slope).astype(LOW)
    in_ref[...] = wide_dot(hidden_grad, up, 1, 1).astype(in_ref.dtype)


def expert_rows(rows, grads, up, down, out_type, in_type):
    count, width = rows.shape
    hidden = up.shape[1]
    return pl.pallas_call(
        expert_kernel,
        out_shape=(
            jax.ShapeDtypeStruct((count, width), out_type),
            jax.ShapeDtypeStruct((count, width), in_type),
            jax.ShapeDtypeStruct((count, hidden), LOW),
        ),
        in_specs=in_vmem(4),
        out_specs=tuple(in_vmem(3)),
        compiler_params=pltpu.CompilerParams(vmem_limit_bytes=VMEM_BYTES),
        cost_estimate=cost(8 * count * width * hidden, 4 * width * hidden + 14 * count * width),
    )(rows, grads, up, down)


def grad_kernel(pairs, *refs):
    total = None
    for k in range(pairs):
        term = wide_dot(refs[k][...], refs[pairs + k][...], 0, 0)
        total = term if total is None else total + term
    refs[2 * pairs][...] = total.astype(LOW)


def outer_sum(acts, grads):
    count, hidden = acts[0].shape
    width = grads[0].shape[1]
    pairs = len(acts)
    return pl.pallas_call(
        functools.partial(grad_kernel, pairs),
        out_shape=jax.ShapeDtypeStruct((hidden, width), LOW),
        in_specs=in_vmem(2 * pairs),
        out_specs=in_vmem(1)[0],
        compiler_params=pltpu.CompilerParams(vmem_limit_bytes=VMEM_BYTES),
        cost_estimate=cost(2 * pairs * count * width * hidden, 2 * hidden * width),
    )(*acts, *grads)


def all_to_all(value, axes):
    return lax.all_to_all(value, axes, split_axis=0, concat_axis=0, tiled=True)


def sum_everywhere(term):
    near = lax.axis_size(NEAR)
    rest = lax.axis_size(REST)
    depth, width = term.shape
    part = jnp.sum(all_to_all(term.reshape(near, depth // near, width), NEAR), axis=0)
    parts = jnp.broadcast_to(part.astype(LOW)[None], (rest,) + part.shape)
    part = jnp.sum(all_to_all(parts, REST).astype(WIDE), axis=0)
    whole = all_to_all(jnp.broadcast_to(part[None], (near,) + part.shape), NEAR)
    return whole.reshape(depth, width)


def shards(tokens, router, up_weight, down_weight, cotangent):
    tokens, cotangent = tokens[0], cotangent[0]
    up, down = up_weight[0], down_weight[0]
    dp = lax.axis_size("dp")

    def right(value):
        return lax.ppermute(value, "dp", [(i, (i + 1) % dp) for i in range(dp)])

    def left(value):
        return lax.ppermute(value, "dp", [(i, (i - 1) % dp) for i in range(dp)])

    logits = wide_einsum("md,ds->ms", tokens, router)
    dispatch = jax.nn.softmax(logits, axis=0)
    combine = jax.nn.softmax(logits, axis=1)
    dispatch_low = dispatch.astype(LOW)
    combine_low = combine.astype(LOW)
    slot_inputs = wide_einsum("ms,md->sd", dispatch_low, tokens).astype(LOW)
    slot_cotangent = wide_einsum("ms,md->sd", combine_low, cotangent).astype(LOW)

    sent = jnp.stack([slot_inputs, slot_cotangent], axis=1)
    own_slots = all_to_all(sent, EXPERT)
    own_rows, own_grads = own_slots[:, 0], own_slots[:, 1]

    left_rows, right_grads = right(own_rows), left(own_grads)
    left_grads, right_rows = right(own_grads), left(own_rows)
    far_rows, far_grads = right(left_rows), left(right_grads)

    own_out, own_in, own_act = expert_rows(own_rows, own_grads, up, down, WIDE, WIDE)
    right_out, right_in, right_act = expert_rows(right_rows, right_grads, up, down, WIDE, LOW)
    left_out, left_in, left_act = expert_rows(left_rows, left_grads, up, down, LOW, WIDE)
    from_left_in, from_right_out = right(right_in), left(left_out)
    far_out, far_in, far_act = expert_rows(far_rows, far_grads, up, down, LOW, LOW)
    via_left, via_right = right(far_out), left(far_in)
    grad_down = outer_sum(
        (own_act, right_act, left_act, far_act), (own_grads, right_grads, left_grads, far_grads)
    )
    from_left_out = right((right_out + via_left.astype(WIDE)).astype(LOW))
    from_right_in = left((left_in + via_right.astype(WIDE)).astype(LOW))
    summed_out = own_out + from_left_out.astype(WIDE) + from_right_out.astype(WIDE)
    summed_in = own_in + from_left_in.astype(WIDE) + from_right_in.astype(WIDE)

    back = all_to_all(jnp.stack([summed_out.astype(LOW), summed_in.astype(LOW)], axis=1), EXPERT)
    slot_outputs, input_grads = back[:, 0], back[:, 1]

    combine_grad = wide_einsum("md,sd->ms", cotangent, slot_outputs)
    dispatch_grad = wide_einsum("md,sd->ms", tokens, input_grads)
    logit_grad = combine * (combine_grad - jnp.sum(combine * combine_grad, axis=1, keepdims=True))
    logit_grad = logit_grad + dispatch * (
        dispatch_grad - jnp.sum(dispatch * dispatch_grad, axis=0, keepdims=True)
    )
    logit_low = logit_grad.astype(LOW)
    grad_router = sum_everywhere(wide_einsum("md,ms->ds", tokens, logit_low))

    grad_tokens = wide_einsum("ms,sd->md", dispatch_low, input_grads)
    grad_tokens = grad_tokens + wide_einsum("ms,ds->md", logit_low, router)
    return (grad_tokens.astype(LOW)[None], grad_router, grad_down[None])


def solution(mesh):
    fine = Mesh(mesh.devices.reshape((-1,) + tuple(EXPERT_SPLIT.values())), EVERY)
    placed = (P(EVERY, None, None), P(), P(EXPERT, None, "dp"), P(EXPERT, "dp", None), P(EVERY, None, None))
    return jax.shard_map(
        shards,
        mesh=fine,
        in_specs=placed,
        out_specs=(P(EVERY, None, None), P(), P(EXPERT, "dp", None)),
        check_vma=False,
    )
```

```python
import math

import jax
import jax.numpy as jnp
from jax import lax
from jax.experimental import pallas as pl
from jax.experimental.pallas import tpu as pltpu
from jax.sharding import Mesh
from jax.sharding import PartitionSpec as P

GELU_SCALE = math.sqrt(2.0 / math.pi)
GELU_CUBIC = 0.044715
LOW = jnp.bfloat16
WIDE = jnp.float32
DP_SPLIT = {"gh": 2, "gl": 2}
EXPERT_SPLIT = {"yl": 2, "xh": 2, "xl": 2, "zh": 4, "zl": 2, "core": 2}
DP = tuple(DP_SPLIT)
EXPERT = tuple(EXPERT_SPLIT)
EVERY = DP + EXPERT
TEAM = ("xl", "core")
ROUTE = ("yl", "xh", "gh", "zh", "zl", "gl")
NEAR = ("yl", "xh", "xl", "zl", "core")
REST = ("gh", "gl", "zh")
VMEM_BYTES = 48 * 2**20


def wide_einsum(spec, left, right):
    return jnp.einsum(spec, left, right, preferred_element_type=WIDE)


def wide_dot(left, right, left_dim, right_dim):
    return lax.dot_general(
        left, right, (((left_dim,), (right_dim,)), ((), ())), preferred_element_type=WIDE
    )


def in_vmem(count):
    return [pl.BlockSpec(memory_space=pltpu.VMEM)] * count


def cost(flops, bytes_accessed):
    return pl.CostEstimate(flops=flops, bytes_accessed=bytes_accessed, transcendentals=0)


def expert_kernel(first_ref, second_ref, up_ref, down_ref, kept_ref, sent_ref, act_ref):
    up, down = up_ref[...], down_ref[...]
    rows = jnp.concatenate([first_ref[0], second_ref[0]])
    hidden_pre = wide_dot(rows, up, 1, 0)
    squared = hidden_pre * hidden_pre
    inner = jnp.tanh(GELU_SCALE * (hidden_pre + GELU_CUBIC * squared * hidden_pre))
    half = 0.5 * (1.0 + inner)
    activation = (hidden_pre * half).astype(LOW)
    act_ref[...] = activation
    outputs = wide_dot(activation, down, 1, 0)
    slope = half + 0.5 * hidden_pre * (1.0 - inner * inner) * (
        GELU_SCALE + 3.0 * GELU_SCALE * GELU_CUBIC * squared
    )
    grads = jnp.concatenate([first_ref[1], second_ref[1]])
    upstream = wide_dot(grads, down, 1, 1)
    hidden_grad = (upstream * slope).astype(LOW)
    input_grads = wide_dot(hidden_grad, up, 1, 1)
    count = kept_ref.shape[1]
    for route, result in enumerate((outputs, input_grads)):
        kept_ref[route] = result[:count].astype(kept_ref.dtype)
        sent_ref[route] = result[count:].astype(sent_ref.dtype)


def expert_rows(first, second, up, down):
    _, count, width = first.shape
    hidden = up.shape[1]
    return pl.pallas_call(
        expert_kernel,
        out_shape=(
            jax.ShapeDtypeStruct(first.shape, WIDE),
            jax.ShapeDtypeStruct(first.shape, LOW),
            jax.ShapeDtypeStruct((2 * count, hidden), LOW),
        ),
        in_specs=in_vmem(4),
        out_specs=tuple(in_vmem(3)),
        compiler_params=pltpu.CompilerParams(vmem_limit_bytes=VMEM_BYTES),
        cost_estimate=cost(16 * count * width * hidden, 4 * width * hidden + 28 * count * width),
    )(first, second, up, down)


def grad_kernel(near_act_ref, far_act_ref, *refs):
    *row_refs, grad_ref = refs
    grads = [ref[1] for ref in row_refs]
    total = wide_dot(near_act_ref[...], jnp.concatenate(grads[:2]), 0, 0)
    total = total + wide_dot(far_act_ref[...], jnp.concatenate(grads[2:]), 0, 0)
    grad_ref[...] = total.astype(LOW)


def outer_sum(near_act, far_act, *blocks):
    count, hidden = near_act.shape
    width = blocks[0].shape[2]
    return pl.pallas_call(
        grad_kernel,
        out_shape=jax.ShapeDtypeStruct((hidden, width), LOW),
        in_specs=in_vmem(6),
        out_specs=in_vmem(1)[0],
        compiler_params=pltpu.CompilerParams(vmem_limit_bytes=VMEM_BYTES),
        cost_estimate=cost(4 * count * width * hidden, 2 * hidden * width),
    )(near_act, far_act, *blocks)


def all_to_all(value, axes):
    return lax.all_to_all(value, axes, split_axis=0, concat_axis=0, tiled=True)


def sum_everywhere(term):
    near = lax.axis_size(NEAR)
    rest = lax.axis_size(REST)
    depth, width = term.shape
    part = jnp.sum(all_to_all(term.reshape(near, depth // near, width), NEAR), axis=0)
    part = jnp.sum(all_to_all(jnp.broadcast_to(part[None], (rest,) + part.shape), REST), axis=0)
    whole = all_to_all(jnp.broadcast_to(part[None], (near,) + part.shape), NEAR)
    return whole.reshape(depth, width)


def swap(value, axis):
    return lax.ppermute(value, axis, [(0, 1), (1, 0)])


def slab_place(slab, team):
    slabs = lax.axis_size(DP)
    return (slab % slabs) * slabs + team % slabs


def move_weights(value, way):
    slabs = lax.axis_size(DP)
    moves = []
    for slab in range(slabs):
        for team in range(slabs):
            if (team - slab) % slabs == 2:
                moves.append((slab_place(slab, team), slab_place(slab + way, slab + way)))
            elif team != slab:
                moves.append((slab_place(slab, team), slab_place(team, slab)))
    return lax.ppermute(value, DP + TEAM, moves)


def finish_move(value, once, way):
    slabs = lax.axis_size(DP)
    moves = [(slab_place(k, k), slab_place(k + way, k - way)) for k in range(slabs)]
    twice = lax.ppermute(once, DP + TEAM, moves)
    offset = (lax.axis_index(TEAM) - lax.axis_index(DP)) % slabs
    return jnp.where(offset == 0, value, jnp.where(offset == 2, twice, once))


def move_back(value):
    slabs = lax.axis_size(DP)
    swaps = [(a * slabs + b, b * slabs + a) for a in range(slabs) for b in range(slabs)]
    return lax.ppermute(value, DP + TEAM, swaps)


def shards(tokens, router, up_weight, down_weight, cotangent):
    tokens, cotangent = tokens[0], cotangent[0]
    up_once = move_weights(up_weight[0], 1)
    down_once = move_weights(down_weight[0], -1)

    logits = wide_einsum("md,ds->ms", tokens, router)
    dispatch = jax.nn.softmax(logits, axis=0)
    combine = jax.nn.softmax(logits, axis=1)
    dispatch_low = dispatch.astype(LOW)
    combine_low = combine.astype(LOW)
    slot_inputs = wide_einsum("ms,md->sd", dispatch_low, tokens).astype(LOW)
    slot_cotangent = wide_einsum("ms,md->sd", combine_low, cotangent).astype(LOW)

    sent = jnp.stack([slot_inputs, slot_cotangent], axis=1)
    own, up_once, down_once = lax.optimization_barrier((all_to_all(sent, ROUTE), up_once, down_once))
    own = jnp.swapaxes(own, 0, 1)
    beside = swap(own, "core")
    across = swap(own, "xl")
    corner = swap(across, "core")

    up = finish_move(up_weight[0], up_once, 1)
    down = finish_move(down_weight[0], down_once, -1)
    far_kept, far_sent, far_act = expert_rows(across, corner, up, down)
    far_back = swap(far_sent, "core")
    own_kept, own_sent, own_act = expert_rows(own, beside, up, down)
    own_back = swap(own_sent, "core")
    across_back = swap((far_kept + far_back.astype(WIDE)).astype(LOW), "xl")
    grad_down = move_back(outer_sum(own_act, far_act, own, beside, across, corner))
    summed = (own_kept + own_back.astype(WIDE) + across_back.astype(WIDE)).astype(LOW)

    back = all_to_all(jnp.swapaxes(summed, 0, 1), ROUTE)
    slot_outputs, input_grads = back[:, 0], back[:, 1]

    combine_grad = wide_einsum("md,sd->ms", cotangent, slot_outputs)
    dispatch_grad = wide_einsum("md,sd->ms", tokens, input_grads)
    logit_grad = combine * (combine_grad - jnp.sum(combine * combine_grad, axis=1, keepdims=True))
    logit_grad = logit_grad + dispatch * (
        dispatch_grad - jnp.sum(dispatch * dispatch_grad, axis=0, keepdims=True)
    )
    logit_low = logit_grad.astype(LOW)
    grad_router = sum_everywhere(wide_einsum("md,ms->ds", tokens, logit_low))

    grad_tokens = wide_einsum("ms,sd->md", dispatch_low, input_grads)
    grad_tokens = grad_tokens + wide_einsum("ms,ds->md", logit_low, router)
    return (grad_tokens.astype(LOW)[None], grad_router, grad_down[None])


def solution(mesh):
    sizes = tuple(DP_SPLIT.values()) + tuple(EXPERT_SPLIT.values())
    images = P(EVERY, None, None)
    return jax.shard_map(
        shards,
        mesh=Mesh(mesh.devices.reshape(sizes), EVERY),
        in_specs=(images, P(), P(EXPERT, None, DP), P(EXPERT, DP, None), images),
        out_specs=(images, P(), P(EXPERT, DP, None)),
        check_vma=False,
    )
```

```python
import functools
import math

import jax
import jax.numpy as jnp
from jax import lax
from jax.experimental import pallas as pl
from jax.experimental.pallas import tpu as pltpu
from jax.sharding import Mesh
from jax.sharding import PartitionSpec as P

GELU_SCALE = math.sqrt(2.0 / math.pi)
GELU_CUBIC = 0.044715
LOW = jnp.bfloat16
WIDE = jnp.float32
DP_SPLIT = {"gh": 2, "gl": 2}
EXPERT_SPLIT = {"yl": 2, "x": 4, "zh": 4, "zl": 2, "core": 2}
DP = tuple(DP_SPLIT)
EXPERT = tuple(EXPERT_SPLIT)
EVERY = DP + EXPERT
TEAM = ("yl", "core")
ROUTE = ("gl", "x", "zh", "zl", "gh")
NEAR = ("yl", "x", "zl", "core")
REST = ("gh", "gl", "zh")
VMEM_BYTES = 48 * 2**20


def wide_einsum(spec, left, right):
    return jnp.einsum(spec, left, right, preferred_element_type=WIDE)


def wide_dot(left, right, left_dim, right_dim):
    return lax.dot_general(
        left, right, (((left_dim,), (right_dim,)), ((), ())), preferred_element_type=WIDE
    )


def in_vmem(count):
    return [pl.BlockSpec(memory_space=pltpu.VMEM)] * count


def cost(flops, bytes_accessed):
    return pl.CostEstimate(flops=flops, bytes_accessed=bytes_accessed, transcendentals=0)


def hidden_kernel(*refs):
    *row_refs, up_ref, act_ref, slope_ref, grad_ref = refs
    hidden_pre = wide_dot(jnp.concatenate([ref[0] for ref in row_refs]), up_ref[...], 1, 0)
    squared = hidden_pre * hidden_pre
    inner = jnp.tanh(GELU_SCALE * (hidden_pre + GELU_CUBIC * squared * hidden_pre))
    half = 0.5 * (1.0 + inner)
    activation = (hidden_pre * half).astype(LOW)
    act_ref[...] = activation
    slope_ref[...] = half + 0.5 * hidden_pre * (1.0 - inner * inner) * (
        GELU_SCALE + 3.0 * GELU_SCALE * GELU_CUBIC * squared
    )
    grads = jnp.concatenate([ref[1] for ref in row_refs])
    grad_ref[...] = wide_dot(activation, grads, 0, 0).astype(LOW)


def hidden_rows(blocks, up):
    _, count, width = blocks[0].shape
    count *= len(blocks)
    hidden = up.shape[1]
    return pl.pallas_call(
        hidden_kernel,
        out_shape=(
            jax.ShapeDtypeStruct((count, hidden), LOW),
            jax.ShapeDtypeStruct((count, hidden), WIDE),
            jax.ShapeDtypeStruct((hidden, width), LOW),
        ),
        in_specs=in_vmem(len(blocks) + 1),
        out_specs=tuple(in_vmem(3)),
        compiler_params=pltpu.CompilerParams(vmem_limit_bytes=VMEM_BYTES),
        cost_estimate=cost(4 * count * width * hidden, 4 * width * hidden + 10 * count * width),
    )(*blocks, up)


def result_kernel(half, first_ref, second_ref, act_ref, slope_ref, up_ref, down_ref, kept_ref, sent_ref):
    count = kept_ref.shape[1]
    here = pl.ds(half * 2 * count, 2 * count)
    down = down_ref[...]
    upstream = wide_dot(jnp.concatenate([first_ref[1], second_ref[1]]), down, 1, 1)
    hidden_grad = (upstream * slope_ref[here, :]).astype(LOW)
    outputs = wide_dot(act_ref[here, :], down, 1, 0)
    input_grads = wide_dot(hidden_grad, up_ref[...], 1, 1)
    for route, result in enumerate((outputs, input_grads)):
        kept_ref[route] = result[:count].astype(kept_ref.dtype)
        sent_ref[route] = result[count:].astype(sent_ref.dtype)


def result_rows(half, first, second, act, slope, up, down):
    _, count, width = first.shape
    hidden = up.shape[1]
    return pl.pallas_call(
        functools.partial(result_kernel, half),
        out_shape=(
            jax.ShapeDtypeStruct(first.shape, WIDE),
            jax.ShapeDtypeStruct(first.shape, LOW),
        ),
        in_specs=in_vmem(6),
        out_specs=tuple(in_vmem(2)),
        compiler_params=pltpu.CompilerParams(vmem_limit_bytes=VMEM_BYTES),
        cost_estimate=cost(12 * count * width * hidden, 4 * width * hidden + 28 * count * width),
    )(first, second, act, slope, up, down)


def all_to_all(value, axes):
    return lax.all_to_all(value, axes, split_axis=0, concat_axis=0, tiled=True)


def sum_everywhere(term):
    near = lax.axis_size(NEAR)
    rest = lax.axis_size(REST)
    depth, width = term.shape
    part = jnp.sum(all_to_all(term.reshape(near, depth // near, width), NEAR), axis=0)
    part = jnp.sum(all_to_all(jnp.broadcast_to(part[None], (rest,) + part.shape), REST), axis=0)
    whole = all_to_all(jnp.broadcast_to(part[None], (near,) + part.shape), NEAR)
    return whole.reshape(depth, width)


def swap(value, axis):
    return lax.ppermute(value, axis, [(0, 1), (1, 0)])


def team_moves():
    moves = []
    for slab in range(4):
        low, odd = slab // 2, slab % 2
        others = ((slab - 1, 0), (slab + 1, 1))
        placed = {slab: (odd, low)}
        for quarter, yl in others + ((slab + 2, 1 - odd),):
            taken = set(placed.values())
            core = low if (yl, low) not in taken else 1 - low
            placed[quarter % 4] = (yl, core)
        for quarter, (yl, core) in placed.items():
            moves.append(((quarter * 2 + odd) * 2 + low, (slab * 2 + yl) * 2 + core))
    return moves


def move(value, moves):
    return lax.ppermute(value, DP + TEAM, moves)


def shards(tokens, router, up_weight, down_weight, cotangent):
    tokens, cotangent = tokens[0], cotangent[0]
    moves = team_moves()
    up = move(up_weight[0], moves)

    logits = wide_einsum("md,ds->ms", tokens, router)
    dispatch = jax.nn.softmax(logits, axis=0)
    combine = jax.nn.softmax(logits, axis=1)
    dispatch_low = dispatch.astype(LOW)
    combine_low = combine.astype(LOW)
    slot_inputs = wide_einsum("ms,md->sd", dispatch_low, tokens).astype(LOW)
    slot_cotangent = wide_einsum("ms,md->sd", combine_low, cotangent).astype(LOW)

    sent = jnp.stack([slot_inputs, slot_cotangent], axis=1)
    own, down = lax.optimization_barrier((all_to_all(sent, ROUTE), down_weight[0]))
    own = jnp.swapaxes(own, 0, 1)
    beside = swap(own, "core")
    across = swap(own, "yl")
    down = move(down, moves)
    corner = swap(across, "core")

    act, slope, grad_down = hidden_rows((across, corner, own, beside), up)
    far_kept, far_sent = result_rows(0, across, corner, act, slope, up, down)
    far_back = swap(far_sent, "core")
    own_kept, own_sent = result_rows(1, own, beside, act, slope, up, down)
    own_back = swap(own_sent, "core")
    across_back = swap((far_kept + far_back.astype(WIDE)).astype(LOW), "yl")
    grad_down, _ = lax.optimization_barrier((grad_down, own_sent))
    grad_down = move(grad_down, [(there, here) for here, there in moves])
    summed = (own_kept + own_back.astype(WIDE) + across_back.astype(WIDE)).astype(LOW)

    back = all_to_all(jnp.swapaxes(summed, 0, 1), ROUTE)
    slot_outputs, input_grads = back[:, 0], back[:, 1]

    combine_grad = wide_einsum("md,sd->ms", cotangent, slot_outputs)
    dispatch_grad = wide_einsum("md,sd->ms", tokens, input_grads)
    logit_grad = combine * (combine_grad - jnp.sum(combine * combine_grad, axis=1, keepdims=True))
    logit_grad = logit_grad + dispatch * (
        dispatch_grad - jnp.sum(dispatch * dispatch_grad, axis=0, keepdims=True)
    )
    logit_low = logit_grad.astype(LOW)
    grad_router = sum_everywhere(wide_einsum("md,ms->ds", tokens, logit_low))

    grad_tokens = wide_einsum("ms,sd->md", dispatch_low, input_grads)
    grad_tokens = grad_tokens + wide_einsum("ms,ds->md", logit_low, router)
    return (grad_tokens.astype(LOW)[None], grad_router, grad_down[None])


def solution(mesh):
    sizes = tuple(DP_SPLIT.values()) + tuple(EXPERT_SPLIT.values())
    images = P(EVERY, None, None)
    return jax.shard_map(
        shards,
        mesh=Mesh(mesh.devices.reshape(sizes), EVERY),
        in_specs=(images, P(), P(EXPERT, None, DP), P(EXPERT, DP, None), images),
        out_specs=(images, P(), P(EXPERT, DP, None)),
        check_vma=False,
    )
```

```python
import math

import jax
import jax.numpy as jnp
from jax import lax
from jax.experimental import pallas as pl
from jax.experimental.pallas import tpu as pltpu
from jax.sharding import Mesh
from jax.sharding import PartitionSpec as P

GELU_SCALE = math.sqrt(2.0 / math.pi)
GELU_CUBIC = 0.044715
LOW = jnp.bfloat16
WIDE = jnp.float32
EXPERT_SPLIT = {"yl": 2, "x": 4, "zh": 4, "zl": 2, "core": 2}
EXPERT = tuple(EXPERT_SPLIT)
EVERY = ("dp",) + EXPERT
NEAR = ("yl", "x", "zl", "core")
REST = ("dp", "zh")
VMEM_BYTES = 48 * 2**20


def wide_einsum(spec, left, right):
    return jnp.einsum(spec, left, right, preferred_element_type=WIDE)


def wide_dot(left, right, left_dim, right_dim):
    return lax.dot_general(
        left, right, (((left_dim,), (right_dim,)), ((), ())), preferred_element_type=WIDE
    )


def in_vmem(count):
    return [pl.BlockSpec(memory_space=pltpu.VMEM)] * count


def cost(flops, bytes_accessed):
    return pl.CostEstimate(flops=flops, bytes_accessed=bytes_accessed, transcendentals=0)


def expert_kernel(rows_ref, up_ref, down_ref, share_ref, act_ref):
    up, down = up_ref[...], down_ref[...]
    hidden_pre = wide_dot(rows_ref[0], up, 1, 0)
    squared = hidden_pre * hidden_pre
    inner = jnp.tanh(GELU_SCALE * (hidden_pre + GELU_CUBIC * squared * hidden_pre))
    half = 0.5 * (1.0 + inner)
    activation = (hidden_pre * half).astype(LOW)
    act_ref[...] = activation
    share_ref[0] = wide_dot(activation, down, 1, 0).astype(LOW)
    slope = half + 0.5 * hidden_pre * (1.0 - inner * inner) * (
        GELU_SCALE + 3.0 * GELU_SCALE * GELU_CUBIC * squared
    )
    upstream = wide_dot(rows_ref[1], down, 1, 1)
    hidden_grad = (upstream * slope).astype(LOW)
    share_ref[1] = wide_dot(hidden_grad, up, 1, 1).astype(LOW)


def expert_rows(rows, up, down):
    _, count, width = rows.shape
    hidden = up.shape[1]
    return pl.pallas_call(
        expert_kernel,
        out_shape=(
            jax.ShapeDtypeStruct(rows.shape, LOW),
            jax.ShapeDtypeStruct((count, hidden), LOW),
        ),
        in_specs=in_vmem(3),
        out_specs=tuple(in_vmem(2)),
        compiler_params=pltpu.CompilerParams(vmem_limit_bytes=VMEM_BYTES),
        cost_estimate=cost(8 * count * width * hidden, 4 * width * hidden + 10 * count * width),
    )(rows, up, down)


def outer_kernel(act_ref, rows_ref, grad_ref):
    grad_ref[...] = wide_dot(act_ref[...], rows_ref[1], 0, 0).astype(LOW)


def outer_sum(act, rows):
    count, hidden = act.shape
    width = rows.shape[2]
    return pl.pallas_call(
        outer_kernel,
        out_shape=jax.ShapeDtypeStruct((hidden, width), LOW),
        in_specs=in_vmem(2),
        out_specs=in_vmem(1)[0],
        compiler_params=pltpu.CompilerParams(vmem_limit_bytes=VMEM_BYTES),
        cost_estimate=cost(2 * count * width * hidden, 2 * hidden * width),
    )(act, rows)


def all_to_all(value, axes):
    return lax.all_to_all(value, axes, split_axis=0, concat_axis=0, tiled=True)


def sum_everywhere(term):
    near = lax.axis_size(NEAR)
    rest = lax.axis_size(REST)
    depth, width = term.shape
    part = jnp.sum(all_to_all(term.reshape(near, depth // near, width), NEAR), axis=0)
    part = jnp.sum(all_to_all(jnp.broadcast_to(part[None], (rest,) + part.shape), REST), axis=0)
    whole = all_to_all(jnp.broadcast_to(part[None], (near,) + part.shape), NEAR)
    return whole.reshape(depth, width)


def shards(tokens, router, up_weight, down_weight, cotangent):
    tokens, cotangent = tokens[0], cotangent[0]
    up, down = up_weight[0], down_weight[0]
    slabs = lax.axis_size("dp")

    logits = wide_einsum("md,ds->ms", tokens, router)
    dispatch = jax.nn.softmax(logits, axis=0)
    combine = jax.nn.softmax(logits, axis=1)
    dispatch_low = dispatch.astype(LOW)
    combine_low = combine.astype(LOW)
    slot_inputs = wide_einsum("ms,md->sd", dispatch_low, tokens).astype(LOW)
    slot_cotangent = wide_einsum("ms,md->sd", combine_low, cotangent).astype(LOW)

    sent = jnp.stack([slot_inputs, slot_cotangent], axis=1)
    copies = jnp.broadcast_to(sent[None], (slabs,) + sent.shape).reshape((-1,) + sent.shape[1:])
    rows = jnp.swapaxes(all_to_all(copies, EVERY), 0, 1)
    shares, act = expert_rows(rows, up, down)
    grad_down = outer_sum(act, rows)
    back = all_to_all(jnp.swapaxes(shares, 0, 1), EVERY).reshape((slabs,) + sent.shape)
    back = jnp.sum(back.astype(WIDE), axis=0).astype(LOW)
    slot_outputs, input_grads = back[:, 0], back[:, 1]

    combine_grad = wide_einsum("md,sd->ms", cotangent, slot_outputs)
    dispatch_grad = wide_einsum("md,sd->ms", tokens, input_grads)
    logit_grad = combine * (combine_grad - jnp.sum(combine * combine_grad, axis=1, keepdims=True))
    logit_grad = logit_grad + dispatch * (
        dispatch_grad - jnp.sum(dispatch * dispatch_grad, axis=0, keepdims=True)
    )
    logit_low = logit_grad.astype(LOW)
    grad_router = sum_everywhere(wide_einsum("md,ms->ds", tokens, logit_low))

    grad_tokens = wide_einsum("ms,sd->md", dispatch_low, input_grads)
    grad_tokens = grad_tokens + wide_einsum("ms,ds->md", logit_low, router)
    return (grad_tokens.astype(LOW)[None], grad_router, grad_down[None])


def solution(mesh):
    sizes = (-1,) + tuple(EXPERT_SPLIT.values())
    images = P(EVERY, None, None)
    return jax.shard_map(
        shards,
        mesh=Mesh(mesh.devices.reshape(sizes), EVERY),
        in_specs=(images, P(), P(EXPERT, None, "dp"), P(EXPERT, "dp", None), images),
        out_specs=(images, P(), P(EXPERT, "dp", None)),
        check_vma=False,
    )
```

```python
import functools
import math

import jax
import jax.numpy as jnp
from jax import lax
from jax.experimental import pallas as pl
from jax.experimental.pallas import tpu as pltpu
from jax.sharding import Mesh
from jax.sharding import PartitionSpec as P

GELU_SCALE = math.sqrt(2.0 / math.pi)
GELU_CUBIC = 0.044715
LOW = jnp.bfloat16
WIDE = jnp.float32
EXPERT_SPLIT = {"yl": 2, "x": 4, "zh": 4, "zl": 2, "core": 2}
EXPERT = tuple(EXPERT_SPLIT)
EVERY = ("dp",) + EXPERT
NEAR = ("yl", "x", "zl", "core")
REST = ("dp", "zh")
VMEM_BYTES = 48 * 2**20


def wide_dot(left, right, left_dim, right_dim):
    return lax.dot_general(
        left, right, (((left_dim,), (right_dim,)), ((), ())), preferred_element_type=WIDE
    )


def in_vmem(count):
    return [pl.BlockSpec(memory_space=pltpu.VMEM)] * count


def cost(flops, bytes_accessed):
    return pl.CostEstimate(flops=flops, bytes_accessed=bytes_accessed, transcendentals=0)


def routing_kernel(tokens_ref, router_ref, cotangent_ref, dispatch_ref, combine_ref, inputs_ref, grads_ref):
    tokens = tokens_ref[...]
    logits = wide_dot(tokens, router_ref[...], 1, 0)
    powers = jnp.exp(logits - jnp.max(logits, axis=0, keepdims=True))
    dispatch = powers / jnp.sum(powers, axis=0, keepdims=True)
    dispatch_ref[...] = dispatch
    inputs_ref[...] = wide_dot(dispatch.astype(LOW), tokens, 0, 0).astype(LOW)
    powers = jnp.exp(logits - jnp.max(logits, axis=1, keepdims=True))
    combine = powers / jnp.sum(powers, axis=1, keepdims=True)
    combine_ref[...] = combine
    grads_ref[...] = wide_dot(combine.astype(LOW), cotangent_ref[...], 0, 0).astype(LOW)


def routing(tokens, router, cotangent):
    patches, width = tokens.shape
    slots = router.shape[1]
    weights = jax.ShapeDtypeStruct((patches, slots), WIDE)
    rows = jax.ShapeDtypeStruct((slots, width), LOW)
    return pl.pallas_call(
        routing_kernel,
        out_shape=(weights, weights, rows, rows),
        in_specs=in_vmem(3),
        out_specs=tuple(in_vmem(4)),
        compiler_params=pltpu.CompilerParams(vmem_limit_bytes=VMEM_BYTES),
        cost_estimate=cost(6 * patches * width * slots, 4 * patches * width),
    )(tokens, router, cotangent)


def expert_kernel(rows_ref, up_ref, down_ref, share_ref, act_ref):
    up, down = up_ref[...], down_ref[...]
    hidden_pre = wide_dot(rows_ref[0], up, 1, 0)
    squared = hidden_pre * hidden_pre
    inner = jnp.tanh(GELU_SCALE * (hidden_pre + GELU_CUBIC * squared * hidden_pre))
    half = 0.5 * (1.0 + inner)
    activation = (hidden_pre * half).astype(LOW)
    act_ref[...] = activation
    share_ref[0] = wide_dot(activation, down, 1, 0).astype(LOW)
    slope = half + 0.5 * hidden_pre * (1.0 - inner * inner) * (
        GELU_SCALE + 3.0 * GELU_SCALE * GELU_CUBIC * squared
    )
    upstream = wide_dot(rows_ref[1], down, 1, 1)
    hidden_grad = (upstream * slope).astype(LOW)
    share_ref[1] = wide_dot(hidden_grad, up, 1, 1).astype(LOW)


def expert_rows(rows, up, down):
    _, count, width = rows.shape
    hidden = up.shape[1]
    return pl.pallas_call(
        expert_kernel,
        out_shape=(
            jax.ShapeDtypeStruct(rows.shape, LOW),
            jax.ShapeDtypeStruct((count, hidden), LOW),
        ),
        in_specs=in_vmem(3),
        out_specs=tuple(in_vmem(2)),
        compiler_params=pltpu.CompilerParams(vmem_limit_bytes=VMEM_BYTES),
        cost_estimate=cost(8 * count * width * hidden, 4 * width * hidden + 10 * count * width),
    )(rows, up, down)


def outer_kernel(act_ref, rows_ref, grad_ref):
    grad_ref[...] = wide_dot(act_ref[...], rows_ref[1], 0, 0).astype(LOW)


def outer_sum(act, rows):
    count, hidden = act.shape
    width = rows.shape[2]
    return pl.pallas_call(
        outer_kernel,
        out_shape=jax.ShapeDtypeStruct((hidden, width), LOW),
        in_specs=in_vmem(2),
        out_specs=in_vmem(1)[0],
        compiler_params=pltpu.CompilerParams(vmem_limit_bytes=VMEM_BYTES),
        cost_estimate=cost(2 * count * width * hidden, 2 * hidden * width),
    )(act, rows)


def logit_kernel(shares_ref, tokens_ref, cotangent_ref, dispatch_ref, combine_ref, inputs_ref, logit_ref, term_ref):
    slabs = shares_ref.shape[1]

    def total(route):
        terms = [shares_ref[route, k].astype(WIDE) for k in range(slabs)]
        return functools.reduce(jnp.add, terms).astype(LOW)

    tokens = tokens_ref[...]
    dispatch, combine = dispatch_ref[...], combine_ref[...]
    input_grads = total(1)
    inputs_ref[...] = input_grads
    grad = wide_dot(cotangent_ref[...], total(0), 1, 1)
    logit_grad = combine * (grad - jnp.sum(combine * grad, axis=1, keepdims=True))
    grad = wide_dot(tokens, input_grads, 1, 1)
    logit_grad = logit_grad + dispatch * (grad - jnp.sum(dispatch * grad, axis=0, keepdims=True))
    logit_low = logit_grad.astype(LOW)
    logit_ref[...] = logit_low
    term_ref[...] = wide_dot(tokens, logit_low, 0, 0).astype(LOW)


def logit_grads(shares, tokens, cotangent, dispatch, combine):
    patches, width = tokens.shape
    slots = dispatch.shape[1]
    return pl.pallas_call(
        logit_kernel,
        out_shape=(
            jax.ShapeDtypeStruct((slots, width), LOW),
            jax.ShapeDtypeStruct((patches, slots), LOW),
            jax.ShapeDtypeStruct((width, slots), LOW),
        ),
        in_specs=in_vmem(5),
        out_specs=tuple(in_vmem(3)),
        compiler_params=pltpu.CompilerParams(vmem_limit_bytes=VMEM_BYTES),
        cost_estimate=cost(6 * patches * width * slots, 4 * patches * width),
    )(shares, tokens, cotangent, dispatch, combine)


def token_kernel(dispatch_ref, inputs_ref, logit_ref, router_ref, grad_ref):
    grad = wide_dot(dispatch_ref[...].astype(LOW), inputs_ref[...], 1, 0)
    grad_ref[...] = (grad + wide_dot(logit_ref[...], router_ref[...], 1, 1)).astype(LOW)


def token_grads(dispatch, input_grads, logit_low, router):
    patches, slots = dispatch.shape
    width = router.shape[0]
    return pl.pallas_call(
        token_kernel,
        out_shape=jax.ShapeDtypeStruct((patches, width), LOW),
        in_specs=in_vmem(4),
        out_specs=in_vmem(1)[0],
        compiler_params=pltpu.CompilerParams(vmem_limit_bytes=VMEM_BYTES),
        cost_estimate=cost(4 * patches * width * slots, 4 * patches * width),
    )(dispatch, input_grads, logit_low, router)


def total_kernel(parts_ref, copies_ref):
    total = jnp.sum(parts_ref[...].astype(WIDE), axis=0).astype(LOW)
    copies_ref[...] = jnp.broadcast_to(total[None], copies_ref.shape)


def total_copies(parts, copies):
    return pl.pallas_call(
        total_kernel,
        out_shape=jax.ShapeDtypeStruct((copies,) + parts.shape[1:], LOW),
        in_specs=in_vmem(1),
        out_specs=in_vmem(1)[0],
        compiler_params=pltpu.CompilerParams(vmem_limit_bytes=VMEM_BYTES),
    )(parts)


def all_to_all(value, axes):
    return lax.all_to_all(value, axes, split_axis=0, concat_axis=0, tiled=True)


def sum_everywhere(term):
    near = lax.axis_size(NEAR)
    depth, width = term.shape
    parts = all_to_all(term.reshape(near, depth // near, width), NEAR)
    parts = all_to_all(total_copies(parts, lax.axis_size(REST)), REST)
    return all_to_all(total_copies(parts, near), NEAR).reshape(depth, width).astype(WIDE)


def shards(tokens, router, up_weight, down_weight, cotangent):
    tokens, cotangent = tokens[0], cotangent[0]
    up, down = up_weight[0], down_weight[0]
    slabs = lax.axis_size("dp")

    dispatch, combine, slot_inputs, slot_cotangent = routing(tokens, router, cotangent)
    sent = jnp.stack([slot_inputs, slot_cotangent], axis=1)
    copies = jnp.broadcast_to(sent[None], (slabs,) + sent.shape).reshape((-1,) + sent.shape[1:])
    rows = jnp.swapaxes(all_to_all(copies, EVERY), 0, 1)
    shares, act = expert_rows(rows, up, down)
    grad_down = outer_sum(act, rows)
    back = jnp.swapaxes(all_to_all(jnp.swapaxes(shares, 0, 1), EVERY), 0, 1)
    back = back.reshape((2, slabs) + slot_inputs.shape)
    input_grads, logit_low, term = logit_grads(back, tokens, cotangent, dispatch, combine)
    grad_router = sum_everywhere(term)
    grad_tokens = token_grads(dispatch, input_grads, logit_low, router)
    return (grad_tokens[None], grad_router, grad_down[None])


def solution(mesh):
    sizes = (-1,) + tuple(EXPERT_SPLIT.values())
    images = P(EVERY, None, None)
    return jax.shard_map(
        shards,
        mesh=Mesh(mesh.devices.reshape(sizes), EVERY),
        in_specs=(images, P(), P(EXPERT, None, "dp"), P(EXPERT, "dp", None), images),
        out_specs=(images, P(), P(EXPERT, "dp", None)),
        check_vma=False,
    )
```

```python
import functools
import math

import jax
import jax.numpy as jnp
from jax import lax
from jax.experimental import pallas as pl
from jax.experimental.pallas import tpu as pltpu
from jax.sharding import Mesh
from jax.sharding import PartitionSpec as P

GELU_SCALE = math.sqrt(2.0 / math.pi)
GELU_CUBIC = 0.044715
LOW = jnp.bfloat16
WIDE = jnp.float32
EXPERT_SPLIT = {"yl": 2, "x": 4, "zh": 4, "zl": 2, "core": 2}
EXPERT = tuple(EXPERT_SPLIT)
EVERY = ("dp",) + EXPERT
NEAR = ("yl", "x", "zl", "core")
REST = ("dp", "zh")
VMEM_BYTES = 20 * 2**20


def wide_dot(left, right, left_dim, right_dim):
    return lax.dot_general(
        left, right, (((left_dim,), (right_dim,)), ((), ())), preferred_element_type=WIDE
    )


def in_vmem(count):
    return [pl.BlockSpec(memory_space=pltpu.VMEM)] * count


def in_hbm(count):
    return [pl.BlockSpec(memory_space=pltpu.HBM)] * count


def fetch(sources, buffers, sems):
    copies = [pltpu.make_async_copy(*pair, sems.at[k]) for k, pair in enumerate(zip(sources, buffers))]
    for copy in copies:
        copy.start()
    return copies


def buffers_for(*arrays):
    return [pltpu.VMEM(a.shape, a.dtype) for a in arrays] + [pltpu.SemaphoreType.DMA((len(arrays),))]


def cost(flops, bytes_accessed):
    return pl.CostEstimate(flops=flops, bytes_accessed=bytes_accessed, transcendentals=0)


def routing_kernel(
    tokens_hbm, router_hbm, cotangent_hbm, dispatch_ref, combine_ref, inputs_ref, grads_ref,
    tokens_ref, router_ref, cotangent_ref, sems,
):
    copies = fetch(
        (tokens_hbm, router_hbm, cotangent_hbm), (tokens_ref, router_ref, cotangent_ref), sems
    )
    copies[0].wait()
    copies[1].wait()
    tokens = tokens_ref[...]
    logits = wide_dot(tokens, router_ref[...], 1, 0)
    powers = jnp.exp(logits - jnp.max(logits, axis=0, keepdims=True))
    dispatch = powers / jnp.sum(powers, axis=0, keepdims=True)
    dispatch_ref[...] = dispatch
    inputs_ref[...] = wide_dot(dispatch.astype(LOW), tokens, 0, 0).astype(LOW)
    powers = jnp.exp(logits - jnp.max(logits, axis=1, keepdims=True))
    combine = powers / jnp.sum(powers, axis=1, keepdims=True)
    combine_ref[...] = combine
    copies[2].wait()
    grads_ref[...] = wide_dot(combine.astype(LOW), cotangent_ref[...], 0, 0).astype(LOW)


def routing(tokens, router, cotangent):
    patches, width = tokens.shape
    slots = router.shape[1]
    weights = jax.ShapeDtypeStruct((patches, slots), WIDE)
    rows = jax.ShapeDtypeStruct((slots, width), LOW)
    return pl.pallas_call(
        routing_kernel,
        out_shape=(weights, weights, rows, rows),
        in_specs=in_hbm(3),
        out_specs=tuple(in_vmem(4)),
        scratch_shapes=buffers_for(tokens, router, cotangent),
        compiler_params=pltpu.CompilerParams(vmem_limit_bytes=61 * 2**20),
        cost_estimate=cost(6 * patches * width * slots, 4 * patches * width),
    )(tokens, router, cotangent)


def expert_kernel(rows_ref, up_hbm, down_hbm, share_ref, act_ref, up_ref, down_ref, sems):
    copies = fetch((up_hbm, down_hbm), (up_ref, down_ref), sems)
    copies[0].wait()
    up = up_ref[...]
    hidden_pre = wide_dot(rows_ref[0], up, 1, 0)
    squared = hidden_pre * hidden_pre
    inner = jnp.tanh(GELU_SCALE * (hidden_pre + GELU_CUBIC * squared * hidden_pre))
    half = 0.5 * (1.0 + inner)
    activation = (hidden_pre * half).astype(LOW)
    act_ref[...] = activation
    copies[1].wait()
    down = down_ref[...]
    share_ref[0] = wide_dot(activation, down, 1, 0).astype(LOW)
    slope = half + 0.5 * hidden_pre * (1.0 - inner * inner) * (
        GELU_SCALE + 3.0 * GELU_SCALE * GELU_CUBIC * squared
    )
    upstream = wide_dot(rows_ref[1], down, 1, 1)
    hidden_grad = (upstream * slope).astype(LOW)
    share_ref[1] = wide_dot(hidden_grad, up, 1, 1).astype(LOW)


def expert_rows(rows, up, down):
    _, count, width = rows.shape
    hidden = up.shape[1]
    return pl.pallas_call(
        expert_kernel,
        out_shape=(
            jax.ShapeDtypeStruct(rows.shape, LOW),
            jax.ShapeDtypeStruct((count, hidden), LOW),
        ),
        in_specs=in_vmem(1) + in_hbm(2),
        out_specs=tuple(in_vmem(2)),
        scratch_shapes=buffers_for(up, down),
        compiler_params=pltpu.CompilerParams(vmem_limit_bytes=VMEM_BYTES),
        cost_estimate=cost(8 * count * width * hidden, 4 * width * hidden + 10 * count * width),
    )(rows, up, down)


def outer_kernel(act_ref, rows_ref, grad_ref):
    grad_ref[...] = wide_dot(act_ref[...], rows_ref[1], 0, 0).astype(LOW)


def outer_sum(act, rows):
    count, hidden = act.shape
    width = rows.shape[2]
    return pl.pallas_call(
        outer_kernel,
        out_shape=jax.ShapeDtypeStruct((hidden, width), LOW),
        in_specs=in_vmem(2),
        out_specs=in_vmem(1)[0],
        compiler_params=pltpu.CompilerParams(vmem_limit_bytes=VMEM_BYTES),
        cost_estimate=cost(2 * count * width * hidden, 2 * hidden * width),
    )(act, rows)


def logit_kernel(
    shares_ref, tokens_hbm, cotangent_hbm, dispatch_ref, combine_ref, inputs_ref, logit_ref, term_ref,
    tokens_ref, cotangent_ref, sems,
):
    copies = fetch((tokens_hbm, cotangent_hbm), (tokens_ref, cotangent_ref), sems)
    slabs = shares_ref.shape[1]

    def total(route):
        terms = [shares_ref[route, k].astype(WIDE) for k in range(slabs)]
        return functools.reduce(jnp.add, terms).astype(LOW)

    dispatch, combine = dispatch_ref[...], combine_ref[...]
    input_grads = total(1)
    inputs_ref[...] = input_grads
    slot_outputs = total(0)
    copies[0].wait()
    copies[1].wait()
    tokens = tokens_ref[...]
    grad = wide_dot(cotangent_ref[...], slot_outputs, 1, 1)
    logit_grad = combine * (grad - jnp.sum(combine * grad, axis=1, keepdims=True))
    grad = wide_dot(tokens, input_grads, 1, 1)
    logit_grad = logit_grad + dispatch * (grad - jnp.sum(dispatch * grad, axis=0, keepdims=True))
    logit_low = logit_grad.astype(LOW)
    logit_ref[...] = logit_low
    term_ref[...] = wide_dot(tokens, logit_low, 0, 0).astype(LOW)


def logit_grads(shares, tokens, cotangent, dispatch, combine):
    patches, width = tokens.shape
    slots = dispatch.shape[1]
    return pl.pallas_call(
        logit_kernel,
        out_shape=(
            jax.ShapeDtypeStruct((slots, width), LOW),
            jax.ShapeDtypeStruct((patches, slots), LOW),
            jax.ShapeDtypeStruct((width, slots), LOW),
        ),
        in_specs=in_vmem(1) + in_hbm(2) + in_vmem(2),
        out_specs=tuple(in_vmem(3)),
        scratch_shapes=buffers_for(tokens, cotangent),
        compiler_params=pltpu.CompilerParams(vmem_limit_bytes=VMEM_BYTES),
        cost_estimate=cost(6 * patches * width * slots, 4 * patches * width),
    )(shares, tokens, cotangent, dispatch, combine)


def token_kernel(dispatch_ref, inputs_ref, logit_ref, router_ref, grad_ref):
    grad = wide_dot(dispatch_ref[...].astype(LOW), inputs_ref[...], 1, 0)
    grad_ref[...] = (grad + wide_dot(logit_ref[...], router_ref[...], 1, 1)).astype(LOW)


def token_grads(dispatch, input_grads, logit_low, router):
    patches, slots = dispatch.shape
    width = router.shape[0]
    return pl.pallas_call(
        token_kernel,
        out_shape=jax.ShapeDtypeStruct((patches, width), LOW),
        in_specs=in_vmem(4),
        out_specs=in_vmem(1)[0],
        compiler_params=pltpu.CompilerParams(vmem_limit_bytes=VMEM_BYTES),
        cost_estimate=cost(4 * patches * width * slots, 4 * patches * width),
    )(dispatch, input_grads, logit_low, router)


def total_kernel(parts_ref, copies_ref):
    total = jnp.sum(parts_ref[...].astype(WIDE), axis=0).astype(LOW)
    copies_ref[...] = jnp.broadcast_to(total[None], copies_ref.shape)


def total_copies(parts, copies):
    return pl.pallas_call(
        total_kernel,
        out_shape=jax.ShapeDtypeStruct((copies,) + parts.shape[1:], LOW),
        in_specs=in_vmem(1),
        out_specs=in_vmem(1)[0],
        compiler_params=pltpu.CompilerParams(vmem_limit_bytes=VMEM_BYTES),
    )(parts)


def all_to_all(value, axes):
    return lax.all_to_all(value, axes, split_axis=0, concat_axis=0, tiled=True)


def sum_everywhere(term):
    near = lax.axis_size(NEAR)
    depth, width = term.shape
    parts = all_to_all(term.reshape(near, depth // near, width), NEAR)
    parts = all_to_all(total_copies(parts, lax.axis_size(REST)), REST)
    return all_to_all(total_copies(parts, near), NEAR).reshape(depth, width).astype(WIDE)


def shards(tokens, router, up_weight, down_weight, cotangent):
    tokens, cotangent = tokens[0], cotangent[0]
    up, down = up_weight[0], down_weight[0]
    slabs = lax.axis_size("dp")

    dispatch, combine, slot_inputs, slot_cotangent = routing(tokens, router, cotangent)
    sent = jnp.stack([slot_inputs, slot_cotangent], axis=1)
    copies = jnp.broadcast_to(sent[None], (slabs,) + sent.shape).reshape((-1,) + sent.shape[1:])
    rows = jnp.swapaxes(all_to_all(copies, EVERY), 0, 1)
    shares, act = expert_rows(rows, up, down)
    grad_down = outer_sum(act, rows)
    back = jnp.swapaxes(all_to_all(jnp.swapaxes(shares, 0, 1), EVERY), 0, 1)
    back = back.reshape((2, slabs) + slot_inputs.shape)
    input_grads, logit_low, term = logit_grads(back, tokens, cotangent, dispatch, combine)
    grad_router = sum_everywhere(term)
    grad_tokens = token_grads(dispatch, input_grads, logit_low, router)
    return (grad_tokens[None], grad_router, grad_down[None])


def solution(mesh):
    sizes = (-1,) + tuple(EXPERT_SPLIT.values())
    images = P(EVERY, None, None)
    return jax.shard_map(
        shards,
        mesh=Mesh(mesh.devices.reshape(sizes), EVERY),
        in_specs=(images, P(), P(EXPERT, None, "dp"), P(EXPERT, "dp", None), images),
        out_specs=(images, P(), P(EXPERT, "dp", None)),
        check_vma=False,
    )
```

```python
import functools
import math

import jax
import jax.numpy as jnp
from jax import lax
from jax.experimental import pallas as pl
from jax.experimental.pallas import tpu as pltpu
from jax.sharding import Mesh
from jax.sharding import PartitionSpec as P

GELU_SCALE = math.sqrt(2.0 / math.pi)
GELU_CUBIC = 0.044715
LOW = jnp.bfloat16
WIDE = jnp.float32
EXPERT_SPLIT = {"yl": 2, "x": 4, "zh": 4, "zl": 2, "core": 2}
EXPERT = tuple(EXPERT_SPLIT)
EVERY = ("dp",) + EXPERT
NEAR = ("yl", "x", "zl", "core")
REST = ("dp", "zh")
VMEM_BYTES = 20 * 2**20
WHOLE_BYTES = 61 * 2**20


def wide_dot(left, right, left_dim, right_dim):
    return lax.dot_general(
        left, right, (((left_dim,), (right_dim,)), ((), ())), preferred_element_type=WIDE
    )


def in_vmem(count):
    return [pl.BlockSpec(memory_space=pltpu.VMEM)] * count


def in_hbm(count):
    return [pl.BlockSpec(memory_space=pltpu.HBM)] * count


def fetch(sources, buffers, sems):
    copies = [pltpu.make_async_copy(*pair, sems.at[k]) for k, pair in enumerate(zip(sources, buffers))]
    for copy in copies:
        copy.start()
    return copies


def buffers_for(*arrays):
    return [pltpu.VMEM(a.shape, a.dtype) for a in arrays] + [pltpu.SemaphoreType.DMA((len(arrays),))]


def cost(flops, bytes_accessed):
    return pl.CostEstimate(flops=flops, bytes_accessed=bytes_accessed, transcendentals=0)


def routing_kernel(
    tokens_hbm, router_hbm, cotangent_hbm, dispatch_ref, combine_ref, rows_ref,
    tokens_ref, router_ref, cotangent_ref, sems,
):
    copies = fetch(
        (tokens_hbm, router_hbm, cotangent_hbm), (tokens_ref, router_ref, cotangent_ref), sems
    )
    copies[0].wait()
    copies[1].wait()
    tokens = tokens_ref[...]
    logits = wide_dot(tokens, router_ref[...], 1, 0)
    powers = jnp.exp(logits - jnp.max(logits, axis=0, keepdims=True))
    dispatch = powers / jnp.sum(powers, axis=0, keepdims=True)
    dispatch_ref[...] = dispatch
    rows_ref[0] = wide_dot(dispatch.astype(LOW), tokens, 0, 0).astype(LOW)
    powers = jnp.exp(logits - jnp.max(logits, axis=1, keepdims=True))
    combine = powers / jnp.sum(powers, axis=1, keepdims=True)
    combine_ref[...] = combine
    copies[2].wait()
    rows_ref[1] = wide_dot(combine.astype(LOW), cotangent_ref[...], 0, 0).astype(LOW)


def routing(tokens, router, cotangent):
    patches, width = tokens.shape
    slots = router.shape[1]
    weights = jax.ShapeDtypeStruct((patches, slots), WIDE)
    rows = jax.ShapeDtypeStruct((2, slots, width), LOW)
    return pl.pallas_call(
        routing_kernel,
        out_shape=(weights, weights, rows),
        in_specs=in_hbm(3),
        out_specs=tuple(in_vmem(3)),
        scratch_shapes=buffers_for(tokens, router, cotangent),
        compiler_params=pltpu.CompilerParams(vmem_limit_bytes=WHOLE_BYTES),
        cost_estimate=cost(6 * patches * width * slots, 4 * patches * width),
    )(tokens, router, cotangent)


def expert_kernel(rows_ref, up_ref, down_ref, share_ref, act_ref):
    up, down = up_ref[...], down_ref[...]
    hidden_pre = wide_dot(rows_ref[0], up, 1, 0)
    squared = hidden_pre * hidden_pre
    inner = jnp.tanh(GELU_SCALE * (hidden_pre + GELU_CUBIC * squared * hidden_pre))
    half = 0.5 * (1.0 + inner)
    activation = (hidden_pre * half).astype(LOW)
    act_ref[...] = activation
    share_ref[0] = wide_dot(activation, down, 1, 0).astype(LOW)
    slope = half + 0.5 * hidden_pre * (1.0 - inner * inner) * (
        GELU_SCALE + 3.0 * GELU_SCALE * GELU_CUBIC * squared
    )
    upstream = wide_dot(rows_ref[1], down, 1, 1)
    hidden_grad = (upstream * slope).astype(LOW)
    share_ref[1] = wide_dot(hidden_grad, up, 1, 1).astype(LOW)


def expert_rows(rows, up, down):
    _, count, width = rows.shape
    hidden = up.shape[1]
    return pl.pallas_call(
        expert_kernel,
        out_shape=(
            jax.ShapeDtypeStruct(rows.shape, LOW),
            jax.ShapeDtypeStruct((count, hidden), LOW),
        ),
        in_specs=in_vmem(3),
        out_specs=tuple(in_vmem(2)),
        compiler_params=pltpu.CompilerParams(vmem_limit_bytes=VMEM_BYTES),
        cost_estimate=cost(8 * count * width * hidden, 4 * width * hidden + 10 * count * width),
    )(rows, up, down)


def outer_kernel(act_ref, rows_ref, grad_ref):
    grad_ref[...] = wide_dot(act_ref[...], rows_ref[1], 0, 0).astype(LOW)


def outer_sum(act, rows):
    count, hidden = act.shape
    width = rows.shape[2]
    return pl.pallas_call(
        outer_kernel,
        out_shape=jax.ShapeDtypeStruct((hidden, width), LOW),
        in_specs=in_vmem(2),
        out_specs=in_vmem(1)[0],
        compiler_params=pltpu.CompilerParams(vmem_limit_bytes=VMEM_BYTES),
        cost_estimate=cost(2 * count * width * hidden, 2 * hidden * width),
    )(act, rows)


def logit_kernel(
    shares_ref, tokens_ref, cotangent_ref, dispatch_ref, combine_ref, inputs_ref, logit_ref, term_ref
):
    slabs = shares_ref.shape[1]

    def total(route):
        terms = [shares_ref[route, k].astype(WIDE) for k in range(slabs)]
        return functools.reduce(jnp.add, terms).astype(LOW)

    dispatch, combine = dispatch_ref[...], combine_ref[...]
    input_grads = total(1)
    inputs_ref[...] = input_grads
    tokens = tokens_ref[...]
    grad = wide_dot(cotangent_ref[...], total(0), 1, 1)
    logit_grad = combine * (grad - jnp.sum(combine * grad, axis=1, keepdims=True))
    grad = wide_dot(tokens, input_grads, 1, 1)
    logit_grad = logit_grad + dispatch * (grad - jnp.sum(dispatch * grad, axis=0, keepdims=True))
    logit_low = logit_grad.astype(LOW)
    logit_ref[...] = logit_low
    term_ref[...] = wide_dot(tokens, logit_low, 0, 0).astype(LOW)


def logit_grads(shares, tokens, cotangent, dispatch, combine):
    patches, width = tokens.shape
    slots = dispatch.shape[1]
    return pl.pallas_call(
        logit_kernel,
        out_shape=(
            jax.ShapeDtypeStruct((slots, width), LOW),
            jax.ShapeDtypeStruct((patches, slots), LOW),
            jax.ShapeDtypeStruct((width, slots), LOW),
        ),
        in_specs=in_vmem(5),
        out_specs=tuple(in_vmem(3)),
        compiler_params=pltpu.CompilerParams(vmem_limit_bytes=VMEM_BYTES),
        cost_estimate=cost(6 * patches * width * slots, 4 * patches * width),
    )(shares, tokens, cotangent, dispatch, combine)


def token_kernel(dispatch_ref, inputs_ref, logit_ref, router_ref, grad_ref):
    grad = wide_dot(dispatch_ref[...].astype(LOW), inputs_ref[...], 1, 0)
    grad_ref[...] = (grad + wide_dot(logit_ref[...], router_ref[...], 1, 1)).astype(LOW)


def token_grads(dispatch, input_grads, logit_low, router):
    patches, slots = dispatch.shape
    width = router.shape[0]
    return pl.pallas_call(
        token_kernel,
        out_shape=jax.ShapeDtypeStruct((patches, width), LOW),
        in_specs=in_vmem(4),
        out_specs=in_vmem(1)[0],
        compiler_params=pltpu.CompilerParams(vmem_limit_bytes=VMEM_BYTES),
        cost_estimate=cost(4 * patches * width * slots, 4 * patches * width),
    )(dispatch, input_grads, logit_low, router)


def total_kernel(parts_ref, copies_ref):
    total = jnp.sum(parts_ref[...].astype(WIDE), axis=0).astype(LOW)
    copies_ref[...] = jnp.broadcast_to(total[None], copies_ref.shape)


def total_copies(parts, copies):
    return pl.pallas_call(
        total_kernel,
        out_shape=jax.ShapeDtypeStruct((copies,) + parts.shape[1:], LOW),
        in_specs=in_vmem(1),
        out_specs=in_vmem(1)[0],
        compiler_params=pltpu.CompilerParams(vmem_limit_bytes=VMEM_BYTES),
    )(parts)


def all_to_all(value, axes):
    return lax.all_to_all(value, axes, split_axis=0, concat_axis=0, tiled=True)


def sum_everywhere(term):
    near = lax.axis_size(NEAR)
    depth, width = term.shape
    parts = all_to_all(term.reshape(near, depth // near, width), NEAR)
    parts = all_to_all(total_copies(parts, lax.axis_size(REST)), REST)
    return all_to_all(total_copies(parts, near), NEAR).reshape(depth, width).astype(WIDE)


def shards(tokens, router, up_weight, down_weight, cotangent):
    tokens, cotangent = tokens[0], cotangent[0]
    up, down = up_weight[0], down_weight[0]
    slabs = lax.axis_size("dp")

    dispatch, combine, slot_rows = routing(tokens, router, cotangent)

    sent = jnp.swapaxes(slot_rows, 0, 1)
    copies = jnp.broadcast_to(sent[None], (slabs,) + sent.shape).reshape((-1,) + sent.shape[1:])
    rows = jnp.swapaxes(all_to_all(copies, EVERY), 0, 1)
    shares, act = expert_rows(rows, up, down)
    grad_down = outer_sum(act, rows)
    back = jnp.swapaxes(all_to_all(jnp.swapaxes(shares, 0, 1), EVERY), 0, 1)
    back = back.reshape((2, slabs) + slot_rows.shape[1:])
    input_grads, logit_low, term = logit_grads(back, tokens, cotangent, dispatch, combine)
    grad_router = sum_everywhere(term)
    grad_tokens = token_grads(dispatch, input_grads, logit_low, router)
    return (grad_tokens[None], grad_router, grad_down[None])


def solution(mesh):
    sizes = (-1,) + tuple(EXPERT_SPLIT.values())
    images = P(EVERY, None, None)
    return jax.shard_map(
        shards,
        mesh=Mesh(mesh.devices.reshape(sizes), EVERY),
        in_specs=(images, P(), P(EXPERT, None, "dp"), P(EXPERT, "dp", None), images),
        out_specs=(images, P(), P(EXPERT, "dp", None)),
        check_vma=False,
    )
```

```python
import functools
import math

import jax
import jax.numpy as jnp
from jax import lax
from jax.experimental import pallas as pl
from jax.experimental.pallas import tpu as pltpu
from jax.sharding import Mesh
from jax.sharding import PartitionSpec as P

GELU_SCALE = math.sqrt(2.0 / math.pi)
GELU_CUBIC = 0.044715
LOW = jnp.bfloat16
WIDE = jnp.float32
EXPERT_SPLIT = {"yl": 2, "x": 4, "zh": 4, "zl": 2, "core": 2}
EXPERT = tuple(EXPERT_SPLIT)
EVERY = ("dp",) + EXPERT
NEAR = ("yl", "x", "zl", "core")
REST = ("dp", "zh")
VMEM_BYTES = 20 * 2**20
WHOLE_BYTES = 61 * 2**20


def wide_dot(left, right, left_dim, right_dim):
    return lax.dot_general(
        left, right, (((left_dim,), (right_dim,)), ((), ())), preferred_element_type=WIDE
    )


def in_vmem(count):
    return [pl.BlockSpec(memory_space=pltpu.VMEM)] * count


def in_hbm(count):
    return [pl.BlockSpec(memory_space=pltpu.HBM)] * count


def fetch(sources, buffers, sems):
    copies = [pltpu.make_async_copy(*pair, sems.at[k]) for k, pair in enumerate(zip(sources, buffers))]
    for copy in copies:
        copy.start()
    return copies


def buffers_for(*arrays):
    return [pltpu.VMEM(a.shape, a.dtype) for a in arrays] + [pltpu.SemaphoreType.DMA((len(arrays),))]


def cost(flops, bytes_accessed):
    return pl.CostEstimate(flops=flops, bytes_accessed=bytes_accessed, transcendentals=0)


def routing_kernel(
    tokens_hbm, router_hbm, cotangent_hbm, dispatch_ref, combine_ref, rows_ref,
    tokens_ref, router_ref, cotangent_ref, sems,
):
    copies = fetch(
        (tokens_hbm, router_hbm, cotangent_hbm), (tokens_ref, router_ref, cotangent_ref), sems
    )
    copies[0].wait()
    copies[1].wait()
    tokens = tokens_ref[...]
    logits = wide_dot(tokens, router_ref[...], 1, 0)
    powers = jnp.exp(logits - jnp.max(logits, axis=0, keepdims=True))
    dispatch = powers / jnp.sum(powers, axis=0, keepdims=True)
    dispatch_ref[...] = dispatch
    rows_ref[0] = wide_dot(dispatch.astype(LOW), tokens, 0, 0).astype(LOW)
    powers = jnp.exp(logits - jnp.max(logits, axis=1, keepdims=True))
    combine = powers / jnp.sum(powers, axis=1, keepdims=True)
    combine_ref[...] = combine
    copies[2].wait()
    rows_ref[1] = wide_dot(combine.astype(LOW), cotangent_ref[...], 0, 0).astype(LOW)


def routing(tokens, router, cotangent):
    patches, width = tokens.shape
    slots = router.shape[1]
    weights = jax.ShapeDtypeStruct((patches, slots), WIDE)
    rows = jax.ShapeDtypeStruct((2, slots, width), LOW)
    return pl.pallas_call(
        routing_kernel,
        out_shape=(weights, weights, rows),
        in_specs=in_hbm(3),
        out_specs=tuple(in_vmem(3)),
        scratch_shapes=buffers_for(tokens, router, cotangent),
        compiler_params=pltpu.CompilerParams(vmem_limit_bytes=WHOLE_BYTES),
        cost_estimate=cost(6 * patches * width * slots, 4 * patches * width),
    )(tokens, router, cotangent)


def expert_kernel(rows_ref, up_ref, down_ref, share_ref, act_ref):
    up, down = up_ref[...], down_ref[...]
    hidden_pre = wide_dot(rows_ref[0], up, 1, 0)
    squared = hidden_pre * hidden_pre
    inner = jnp.tanh(GELU_SCALE * (hidden_pre + GELU_CUBIC * squared * hidden_pre))
    half = 0.5 * (1.0 + inner)
    activation = (hidden_pre * half).astype(LOW)
    act_ref[...] = activation
    share_ref[0] = wide_dot(activation, down, 1, 0).astype(LOW)
    slope = half + 0.5 * hidden_pre * (1.0 - inner * inner) * (
        GELU_SCALE + 3.0 * GELU_SCALE * GELU_CUBIC * squared
    )
    upstream = wide_dot(rows_ref[1], down, 1, 1)
    hidden_grad = (upstream * slope).astype(LOW)
    share_ref[1] = wide_dot(hidden_grad, up, 1, 1).astype(LOW)


def expert_rows(rows, up, down):
    _, count, width = rows.shape
    hidden = up.shape[1]
    return pl.pallas_call(
        expert_kernel,
        out_shape=(
            jax.ShapeDtypeStruct(rows.shape, LOW),
            jax.ShapeDtypeStruct((count, hidden), LOW),
        ),
        in_specs=in_vmem(3),
        out_specs=tuple(in_vmem(2)),
        compiler_params=pltpu.CompilerParams(vmem_limit_bytes=VMEM_BYTES),
        cost_estimate=cost(8 * count * width * hidden, 4 * width * hidden + 10 * count * width),
    )(rows, up, down)


def outer_kernel(act_ref, rows_ref, grad_ref):
    grad_ref[...] = wide_dot(act_ref[...], rows_ref[1], 0, 0).astype(LOW)


def outer_sum(act, rows):
    count, hidden = act.shape
    width = rows.shape[2]
    return pl.pallas_call(
        outer_kernel,
        out_shape=jax.ShapeDtypeStruct((hidden, width), LOW),
        in_specs=in_vmem(2),
        out_specs=in_vmem(1)[0],
        compiler_params=pltpu.CompilerParams(vmem_limit_bytes=VMEM_BYTES),
        cost_estimate=cost(2 * count * width * hidden, 2 * hidden * width),
    )(act, rows)


def logit_kernel(
    shares_ref, tokens_ref, cotangent_ref, dispatch_ref, combine_ref, inputs_ref, logit_ref, term_ref
):
    slabs = shares_ref.shape[1]

    def total(route):
        terms = [shares_ref[route, k].astype(WIDE) for k in range(slabs)]
        return functools.reduce(jnp.add, terms).astype(LOW)

    dispatch, combine = dispatch_ref[...], combine_ref[...]
    input_grads = total(1)
    inputs_ref[...] = input_grads
    tokens = tokens_ref[...]
    grad = wide_dot(cotangent_ref[...], total(0), 1, 1)
    logit_grad = combine * (grad - jnp.sum(combine * grad, axis=1, keepdims=True))
    grad = wide_dot(tokens, input_grads, 1, 1)
    logit_grad = logit_grad + dispatch * (grad - jnp.sum(dispatch * grad, axis=0, keepdims=True))
    logit_low = logit_grad.astype(LOW)
    logit_ref[...] = logit_low
    term_ref[...] = wide_dot(tokens, logit_low, 0, 0).astype(LOW)


def logit_grads(shares, tokens, cotangent, dispatch, combine):
    patches, width = tokens.shape
    slots = dispatch.shape[1]
    return pl.pallas_call(
        logit_kernel,
        out_shape=(
            jax.ShapeDtypeStruct((slots, width), LOW),
            jax.ShapeDtypeStruct((patches, slots), LOW),
            jax.ShapeDtypeStruct((width, slots), LOW),
        ),
        in_specs=in_vmem(5),
        out_specs=tuple(in_vmem(3)),
        compiler_params=pltpu.CompilerParams(vmem_limit_bytes=VMEM_BYTES),
        cost_estimate=cost(6 * patches * width * slots, 4 * patches * width),
    )(shares, tokens, cotangent, dispatch, combine)


def token_kernel(dispatch_ref, inputs_ref, logit_ref, router_ref, grad_ref):
    grad = wide_dot(dispatch_ref[...].astype(LOW), inputs_ref[...], 1, 0)
    grad_ref[...] = (grad + wide_dot(logit_ref[...], router_ref[...], 1, 1)).astype(LOW)


def token_grads(dispatch, input_grads, logit_low, router):
    patches, slots = dispatch.shape
    width = router.shape[0]
    return pl.pallas_call(
        token_kernel,
        out_shape=jax.ShapeDtypeStruct((patches, width), LOW),
        in_specs=in_vmem(4),
        out_specs=in_vmem(1)[0],
        compiler_params=pltpu.CompilerParams(vmem_limit_bytes=VMEM_BYTES),
        cost_estimate=cost(4 * patches * width * slots, 4 * patches * width),
    )(dispatch, input_grads, logit_low, router)


def total_kernel(parts_ref, copies_ref):
    total = jnp.sum(parts_ref[...].astype(WIDE), axis=0).astype(copies_ref.dtype)
    copies_ref[...] = jnp.broadcast_to(total[None], copies_ref.shape)


def total_copies(parts, copies, kind):
    return pl.pallas_call(
        total_kernel,
        out_shape=jax.ShapeDtypeStruct((copies,) + parts.shape[1:], kind),
        in_specs=in_vmem(1),
        out_specs=in_vmem(1)[0],
        compiler_params=pltpu.CompilerParams(vmem_limit_bytes=VMEM_BYTES),
    )(parts)


def all_to_all(value, axes):
    return lax.all_to_all(value, axes, split_axis=0, concat_axis=0, tiled=True)


def sum_everywhere(term):
    near = lax.axis_size(NEAR)
    depth, width = term.shape
    parts = all_to_all(term.reshape(near, depth // near, width), NEAR)
    parts = all_to_all(total_copies(parts, lax.axis_size(REST), WIDE), REST)
    return all_to_all(total_copies(parts, near, LOW), NEAR).reshape(depth, width).astype(WIDE)


def shards(tokens, router, up_weight, down_weight, cotangent):
    tokens, cotangent = tokens[0], cotangent[0]
    up, down = up_weight[0], down_weight[0]
    slabs = lax.axis_size("dp")

    dispatch, combine, slot_rows = routing(tokens, router, cotangent)

    sent = jnp.swapaxes(slot_rows, 0, 1)
    copies = jnp.broadcast_to(sent[None], (slabs,) + sent.shape).reshape((-1,) + sent.shape[1:])
    rows = jnp.swapaxes(all_to_all(copies, EVERY), 0, 1)
    shares, act = expert_rows(rows, up, down)
    grad_down = outer_sum(act, rows)
    back = jnp.swapaxes(all_to_all(jnp.swapaxes(shares, 0, 1), EVERY), 0, 1)
    back = back.reshape((2, slabs) + slot_rows.shape[1:])
    input_grads, logit_low, term = logit_grads(back, tokens, cotangent, dispatch, combine)
    grad_router = sum_everywhere(term)
    grad_tokens = token_grads(dispatch, input_grads, logit_low, router)
    return (grad_tokens[None], grad_router, grad_down[None])


def solution(mesh):
    sizes = (-1,) + tuple(EXPERT_SPLIT.values())
    images = P(EVERY, None, None)
    return jax.shard_map(
        shards,
        mesh=Mesh(mesh.devices.reshape(sizes), EVERY),
        in_specs=(images, P(), P(EXPERT, None, "dp"), P(EXPERT, "dp", None), images),
        out_specs=(images, P(), P(EXPERT, "dp", None)),
        check_vma=False,
    )
```

```python
import functools
import math

import jax
import jax.numpy as jnp
from jax import lax
from jax.experimental import pallas as pl
from jax.experimental.pallas import tpu as pltpu
from jax.sharding import Mesh
from jax.sharding import PartitionSpec as P

GELU_SCALE = math.sqrt(2.0 / math.pi)
GELU_CUBIC = 0.044715
LOW = jnp.bfloat16
WIDE = jnp.float32
EXPERT_SPLIT = {"yl": 2, "x": 4, "zh": 4, "zl": 2, "core": 2}
EXPERT = tuple(EXPERT_SPLIT)
EVERY = ("dp",) + EXPERT
NEAR = ("yl", "x", "zl", "core")
REST = ("dp", "zh")
COLUMN = ("dp", "yl", "core")
HOSTS = ("dp", "yl", "x", "zh", "zl")
VMEM_BYTES = 20 * 2**20
WHOLE_BYTES = 61 * 2**20


def wide_dot(left, right, left_dim, right_dim):
    return lax.dot_general(
        left, right, (((left_dim,), (right_dim,)), ((), ())), preferred_element_type=WIDE
    )


def in_vmem(count):
    return [pl.BlockSpec(memory_space=pltpu.VMEM)] * count


def in_hbm(count):
    return [pl.BlockSpec(memory_space=pltpu.HBM)] * count


def fetch(sources, buffers, sems):
    copies = [pltpu.make_async_copy(*pair, sems.at[k]) for k, pair in enumerate(zip(sources, buffers))]
    for copy in copies:
        copy.start()
    return copies


def buffers_for(*arrays):
    return [pltpu.VMEM(a.shape, a.dtype) for a in arrays] + [pltpu.SemaphoreType.DMA((len(arrays),))]


def cost(flops, bytes_accessed):
    return pl.CostEstimate(flops=flops, bytes_accessed=bytes_accessed, transcendentals=0)


def routing_kernel(
    tokens_hbm, router_hbm, cotangent_hbm, dispatch_ref, combine_ref, rows_ref,
    tokens_ref, router_ref, cotangent_ref, sems,
):
    copies = fetch(
        (tokens_hbm, router_hbm, cotangent_hbm), (tokens_ref, router_ref, cotangent_ref), sems
    )
    copies[0].wait()
    copies[1].wait()
    tokens = tokens_ref[...]
    logits = wide_dot(tokens, router_ref[...], 1, 0)
    powers = jnp.exp(logits - jnp.max(logits, axis=0, keepdims=True))
    dispatch = powers / jnp.sum(powers, axis=0, keepdims=True)
    dispatch_ref[...] = dispatch
    rows_ref[0] = wide_dot(dispatch.astype(LOW), tokens, 0, 0).astype(LOW)
    powers = jnp.exp(logits - jnp.max(logits, axis=1, keepdims=True))
    combine = powers / jnp.sum(powers, axis=1, keepdims=True)
    combine_ref[...] = combine
    copies[2].wait()
    rows_ref[1] = wide_dot(combine.astype(LOW), cotangent_ref[...], 0, 0).astype(LOW)


def routing(tokens, router, cotangent):
    patches, width = tokens.shape
    slots = router.shape[1]
    weights = jax.ShapeDtypeStruct((patches, slots), WIDE)
    rows = jax.ShapeDtypeStruct((2, slots, width), LOW)
    return pl.pallas_call(
        routing_kernel,
        out_shape=(weights, weights, rows),
        in_specs=in_hbm(3),
        out_specs=tuple(in_vmem(3)),
        scratch_shapes=buffers_for(tokens, router, cotangent),
        compiler_params=pltpu.CompilerParams(vmem_limit_bytes=WHOLE_BYTES),
        cost_estimate=cost(6 * patches * width * slots, 4 * patches * width),
    )(tokens, router, cotangent)


def expert_kernel(rows_ref, up_ref, down_ref, share_ref, act_ref):
    up, down = up_ref[...], down_ref[...]
    hidden_pre = wide_dot(rows_ref[0], up, 1, 0)
    squared = hidden_pre * hidden_pre
    inner = jnp.tanh(GELU_SCALE * (hidden_pre + GELU_CUBIC * squared * hidden_pre))
    half = 0.5 * (1.0 + inner)
    activation = (hidden_pre * half).astype(LOW)
    act_ref[...] = activation
    share_ref[0] = wide_dot(activation, down, 1, 0).astype(share_ref.dtype)
    slope = half + 0.5 * hidden_pre * (1.0 - inner * inner) * (
        GELU_SCALE + 3.0 * GELU_SCALE * GELU_CUBIC * squared
    )
    upstream = wide_dot(rows_ref[1], down, 1, 1)
    hidden_grad = (upstream * slope).astype(LOW)
    share_ref[1] = wide_dot(hidden_grad, up, 1, 1).astype(share_ref.dtype)


def expert_rows(rows, up, down, kind):
    _, count, width = rows.shape
    hidden = up.shape[1]
    return pl.pallas_call(
        expert_kernel,
        out_shape=(
            jax.ShapeDtypeStruct(rows.shape, kind),
            jax.ShapeDtypeStruct((count, hidden), LOW),
        ),
        in_specs=in_vmem(3),
        out_specs=tuple(in_vmem(2)),
        compiler_params=pltpu.CompilerParams(vmem_limit_bytes=VMEM_BYTES),
        cost_estimate=cost(8 * count * width * hidden, 4 * width * hidden + 10 * count * width),
    )(rows, up, down)


def outer_kernel(act_ref, rows_ref, other_act_ref, other_rows_ref, grad_ref):
    total = wide_dot(act_ref[...], rows_ref[1], 0, 0)
    grad_ref[...] = (total + wide_dot(other_act_ref[...], other_rows_ref[1], 0, 0)).astype(LOW)


def outer_sum(act, rows, other_act, other_rows):
    count, hidden = act.shape
    width = rows.shape[2]
    return pl.pallas_call(
        outer_kernel,
        out_shape=jax.ShapeDtypeStruct((hidden, width), LOW),
        in_specs=in_vmem(4),
        out_specs=in_vmem(1)[0],
        compiler_params=pltpu.CompilerParams(vmem_limit_bytes=VMEM_BYTES),
        cost_estimate=cost(4 * count * width * hidden, 2 * hidden * width),
    )(act, rows, other_act, other_rows)


def logit_kernel(
    shares_ref, tokens_ref, cotangent_ref, dispatch_ref, combine_ref, inputs_ref, logit_ref, term_ref
):
    slabs = shares_ref.shape[1]

    def total(route):
        terms = [shares_ref[route, k].astype(WIDE) for k in range(slabs)]
        return functools.reduce(jnp.add, terms).astype(LOW)

    dispatch, combine = dispatch_ref[...], combine_ref[...]
    input_grads = total(1)
    inputs_ref[...] = input_grads
    tokens = tokens_ref[...]
    grad = wide_dot(cotangent_ref[...], total(0), 1, 1)
    logit_grad = combine * (grad - jnp.sum(combine * grad, axis=1, keepdims=True))
    grad = wide_dot(tokens, input_grads, 1, 1)
    logit_grad = logit_grad + dispatch * (grad - jnp.sum(dispatch * grad, axis=0, keepdims=True))
    logit_low = logit_grad.astype(LOW)
    logit_ref[...] = logit_low
    term_ref[...] = wide_dot(tokens, logit_low, 0, 0).astype(LOW)


def logit_grads(shares, tokens, cotangent, dispatch, combine):
    patches, width = tokens.shape
    slots = dispatch.shape[1]
    return pl.pallas_call(
        logit_kernel,
        out_shape=(
            jax.ShapeDtypeStruct((slots, width), LOW),
            jax.ShapeDtypeStruct((patches, slots), LOW),
            jax.ShapeDtypeStruct((width, slots), LOW),
        ),
        in_specs=in_vmem(5),
        out_specs=tuple(in_vmem(3)),
        compiler_params=pltpu.CompilerParams(vmem_limit_bytes=VMEM_BYTES),
        cost_estimate=cost(6 * patches * width * slots, 4 * patches * width),
    )(shares, tokens, cotangent, dispatch, combine)


def token_kernel(dispatch_ref, inputs_ref, logit_ref, router_ref, grad_ref):
    grad = wide_dot(dispatch_ref[...].astype(LOW), inputs_ref[...], 1, 0)
    grad_ref[...] = (grad + wide_dot(logit_ref[...], router_ref[...], 1, 1)).astype(LOW)


def token_grads(dispatch, input_grads, logit_low, router):
    patches, slots = dispatch.shape
    width = router.shape[0]
    return pl.pallas_call(
        token_kernel,
        out_shape=jax.ShapeDtypeStruct((patches, width), LOW),
        in_specs=in_vmem(4),
        out_specs=in_vmem(1)[0],
        compiler_params=pltpu.CompilerParams(vmem_limit_bytes=VMEM_BYTES),
        cost_estimate=cost(4 * patches * width * slots, 4 * patches * width),
    )(dispatch, input_grads, logit_low, router)


def total_kernel(parts_ref, copies_ref):
    total = jnp.sum(parts_ref[...].astype(WIDE), axis=0).astype(copies_ref.dtype)
    copies_ref[...] = jnp.broadcast_to(total[None], copies_ref.shape)


def total_copies(parts, copies, kind):
    return pl.pallas_call(
        total_kernel,
        out_shape=jax.ShapeDtypeStruct((copies,) + parts.shape[1:], kind),
        in_specs=in_vmem(1),
        out_specs=in_vmem(1)[0],
        compiler_params=pltpu.CompilerParams(vmem_limit_bytes=VMEM_BYTES),
    )(parts)


def all_to_all(value, axes):
    return lax.all_to_all(value, axes, split_axis=0, concat_axis=0, tiled=True)


def sum_everywhere(term):
    near = lax.axis_size(NEAR)
    depth, width = term.shape
    parts = all_to_all(term.reshape(near, depth // near, width), NEAR)
    parts = all_to_all(total_copies(parts, lax.axis_size(REST), WIDE), REST)
    return all_to_all(total_copies(parts, near, LOW), NEAR).reshape(depth, width).astype(WIDE)


def host_moves():
    moves = []
    for slab in range(4):
        for yl in range(2):
            for core in range(2):
                place = 2 * slab + yl
                onward = (slab + core) % 2 == 0
                host = (place + (1 if onward else -1)) % 8
                moves.append((2 * place + core, 2 * host + (0 if onward else 1)))
    return moves


def move(value, moves):
    return lax.ppermute(value, COLUMN, moves)


def swap_cores(value):
    return lax.ppermute(value, "core", [(0, 1), (1, 0)])


def to_hosts(rows):
    _, routes, width = rows.shape
    placed = rows.reshape(2, -1, 2, routes, width)
    even = jnp.stack([placed[1, :, 1], placed[0, :, 0]])
    odd = jnp.stack([placed[1, :, 0], placed[0, :, 1]])
    return jnp.stack([even, odd, even, odd]).reshape(-1, routes, width)


def from_hosts(rows):
    _, routes, width = rows.shape
    hosted = rows.reshape(2, 2, 2, -1, routes, width)
    shares = jnp.stack([hosted[:, :, 1], hosted[:, ::-1, 0]], axis=1)
    return shares.transpose(4, 0, 1, 3, 2, 5).reshape(routes, 2, -1, width)


def shards(tokens, router, up_weight, down_weight, cotangent):
    tokens, cotangent = tokens[0], cotangent[0]
    moves = host_moves()
    up, down = move(up_weight[0], moves), move(down_weight[0], moves)

    dispatch, combine, slot_rows = routing(tokens, router, cotangent)

    arrived = all_to_all(to_hosts(jnp.swapaxes(slot_rows, 0, 1)), HOSTS)
    arrived, up, down = lax.optimization_barrier((arrived, up, down))
    rows = jnp.swapaxes(arrived, 0, 1)
    other = swap_cores(rows)
    other_share, other_act = expert_rows(other, up, down, LOW)
    got = swap_cores(other_share)
    share, act = expert_rows(rows, up, down, WIDE)
    grad_down = outer_sum(act, rows, other_act, other)
    shares = (share + got.astype(WIDE)).astype(LOW)
    back = all_to_all(jnp.swapaxes(shares, 0, 1), HOSTS)
    back, grad_down = lax.optimization_barrier((back, grad_down))
    grad_down = move(grad_down, [(there, here) for here, there in moves])
    back = from_hosts(back)
    input_grads, logit_low, term = logit_grads(back, tokens, cotangent, dispatch, combine)
    grad_router = sum_everywhere(term)
    grad_tokens = token_grads(dispatch, input_grads, logit_low, router)
    return (grad_tokens[None], grad_router, grad_down[None])


def solution(mesh):
    sizes = (-1,) + tuple(EXPERT_SPLIT.values())
    images = P(EVERY, None, None)
    return jax.shard_map(
        shards,
        mesh=Mesh(mesh.devices.reshape(sizes), EVERY),
        in_specs=(images, P(), P(EXPERT, None, "dp"), P(EXPERT, "dp", None), images),
        out_specs=(images, P(), P(EXPERT, "dp", None)),
        check_vma=False,
    )
```

```python
import functools
import math

import jax
import jax.numpy as jnp
from jax import lax
from jax.experimental import pallas as pl
from jax.experimental.pallas import tpu as pltpu
from jax.sharding import Mesh
from jax.sharding import PartitionSpec as P

GELU_SCALE = math.sqrt(2.0 / math.pi)
GELU_CUBIC = 0.044715
LOW = jnp.bfloat16
WIDE = jnp.float32
EXPERT_SPLIT = {"yl": 2, "x": 4, "zh": 4, "zl": 2, "core": 2}
EXPERT = tuple(EXPERT_SPLIT)
EVERY = ("dp",) + EXPERT
NEAR = ("yl", "x", "zl", "core")
REST = ("dp", "zh")
COLUMN = ("dp", "yl", "core")
HOSTS = ("dp", "yl", "x", "zh", "zl")
VMEM_BYTES = 20 * 2**20


def wide_dot(left, right, left_dim, right_dim):
    return lax.dot_general(
        left, right, (((left_dim,), (right_dim,)), ((), ())), preferred_element_type=WIDE
    )


def in_vmem(count):
    return [pl.BlockSpec(memory_space=pltpu.VMEM)] * count


def cost(flops, bytes_accessed):
    return pl.CostEstimate(flops=flops, bytes_accessed=bytes_accessed, transcendentals=0)


def host_block(slab, yl):
    return (1 - yl) * 2 + (slab + 1 - yl) % 2


def blocked(slots):
    rest = slots // 4
    slot = lax.broadcasted_iota(jnp.int32, (slots, slots), 0)
    place = lax.broadcasted_iota(jnp.int32, (slots, slots), 1)
    core = place // rest % 2
    here = (place // (2 * rest) * rest + place % rest) * 2 + core
    return jnp.where(slot == here, 1.0, 0.0).astype(LOW)


def routing_kernel(tokens_ref, router_ref, cotangent_ref, dispatch_ref, combine_ref, sent_ref):
    tokens = tokens_ref[...]
    slots = router_ref.shape[1]
    rest = slots // 4
    router = wide_dot(router_ref[...], blocked(slots), 1, 0).astype(LOW)
    logits = wide_dot(tokens, router, 1, 0)
    powers = jnp.exp(logits - jnp.max(logits, axis=0, keepdims=True))
    dispatch = powers / jnp.sum(powers, axis=0, keepdims=True)
    dispatch_ref[...] = dispatch
    inputs = wide_dot(dispatch.astype(LOW), tokens, 0, 0).astype(LOW)
    powers = jnp.exp(logits - jnp.max(logits, axis=1, keepdims=True))
    combine = powers / jnp.sum(powers, axis=1, keepdims=True)
    combine_ref[...] = combine
    grads = wide_dot(combine.astype(LOW), cotangent_ref[...], 0, 0).astype(LOW)
    for route, rows in enumerate((inputs, grads)):
        for chip in range(8):
            block = host_block(chip // 2, chip % 2) * rest
            sent_ref[route, chip * rest : (chip + 1) * rest] = rows[block : block + rest]


def routing(tokens, router, cotangent):
    patches, width = tokens.shape
    slots = router.shape[1]
    weights = jax.ShapeDtypeStruct((patches, slots), WIDE)
    return pl.pallas_call(
        routing_kernel,
        out_shape=(weights, weights, jax.ShapeDtypeStruct((2, 2 * slots, width), LOW)),
        in_specs=in_vmem(3),
        out_specs=tuple(in_vmem(3)),
        compiler_params=pltpu.CompilerParams(vmem_limit_bytes=VMEM_BYTES),
        cost_estimate=cost(6 * patches * width * slots, 4 * patches * width),
    )(tokens, router, cotangent)


def expert_kernel(rows_ref, up_ref, down_ref, share_ref, act_ref):
    up, down = up_ref[...], down_ref[...]
    hidden_pre = wide_dot(rows_ref[0], up, 1, 0)
    squared = hidden_pre * hidden_pre
    inner = jnp.tanh(GELU_SCALE * (hidden_pre + GELU_CUBIC * squared * hidden_pre))
    half = 0.5 * (1.0 + inner)
    activation = (hidden_pre * half).astype(LOW)
    act_ref[...] = activation
    share_ref[0] = wide_dot(activation, down, 1, 0).astype(share_ref.dtype)
    slope = half + 0.5 * hidden_pre * (1.0 - inner * inner) * (
        GELU_SCALE + 3.0 * GELU_SCALE * GELU_CUBIC * squared
    )
    upstream = wide_dot(rows_ref[1], down, 1, 1)
    hidden_grad = (upstream * slope).astype(LOW)
    share_ref[1] = wide_dot(hidden_grad, up, 1, 1).astype(share_ref.dtype)


def expert_rows(rows, up, down, kind):
    _, count, width = rows.shape
    hidden = up.shape[1]
    return pl.pallas_call(
        expert_kernel,
        out_shape=(
            jax.ShapeDtypeStruct(rows.shape, kind),
            jax.ShapeDtypeStruct((count, hidden), LOW),
        ),
        in_specs=in_vmem(3),
        out_specs=tuple(in_vmem(2)),
        compiler_params=pltpu.CompilerParams(vmem_limit_bytes=VMEM_BYTES),
        cost_estimate=cost(8 * count * width * hidden, 4 * width * hidden + 10 * count * width),
    )(rows, up, down)


def outer_kernel(act_ref, rows_ref, other_act_ref, other_rows_ref, grad_ref):
    total = wide_dot(act_ref[...], rows_ref[1], 0, 0)
    grad_ref[...] = (total + wide_dot(other_act_ref[...], other_rows_ref[1], 0, 0)).astype(LOW)


def outer_sum(act, rows, other_act, other_rows):
    count, hidden = act.shape
    width = rows.shape[2]
    return pl.pallas_call(
        outer_kernel,
        out_shape=jax.ShapeDtypeStruct((hidden, width), LOW),
        in_specs=in_vmem(4),
        out_specs=in_vmem(1)[0],
        compiler_params=pltpu.CompilerParams(vmem_limit_bytes=VMEM_BYTES),
        cost_estimate=cost(4 * count * width * hidden, 2 * hidden * width),
    )(act, rows, other_act, other_rows)


def logit_kernel(
    shares_ref, tokens_ref, cotangent_ref, dispatch_ref, combine_ref, inputs_ref, logit_ref, term_ref
):
    slots = dispatch_ref.shape[1]
    rest = slots // 4

    def total(route):
        parts = [None] * 4
        for chip in range(8):
            share = shares_ref[route, chip * rest : (chip + 1) * rest].astype(WIDE)
            block = host_block(chip // 2, chip % 2)
            parts[block] = share if parts[block] is None else parts[block] + share
        return jnp.concatenate([part.astype(LOW) for part in parts])

    tokens = tokens_ref[...]
    dispatch, combine = dispatch_ref[...], combine_ref[...]
    input_grads = total(1)
    inputs_ref[...] = input_grads
    grad = wide_dot(cotangent_ref[...], total(0), 1, 1)
    logit_grad = combine * (grad - jnp.sum(combine * grad, axis=1, keepdims=True))
    grad = wide_dot(tokens, input_grads, 1, 1)
    logit_grad = logit_grad + dispatch * (grad - jnp.sum(dispatch * grad, axis=0, keepdims=True))
    logit_low = wide_dot(logit_grad.astype(LOW), blocked(slots), 1, 1).astype(LOW)
    logit_ref[...] = logit_low
    term_ref[...] = wide_dot(tokens, logit_low, 0, 0).astype(LOW)


def logit_grads(shares, tokens, cotangent, dispatch, combine):
    patches, width = tokens.shape
    slots = dispatch.shape[1]
    return pl.pallas_call(
        logit_kernel,
        out_shape=(
            jax.ShapeDtypeStruct((slots, width), LOW),
            jax.ShapeDtypeStruct((patches, slots), LOW),
            jax.ShapeDtypeStruct((width, slots), LOW),
        ),
        in_specs=in_vmem(5),
        out_specs=tuple(in_vmem(3)),
        compiler_params=pltpu.CompilerParams(vmem_limit_bytes=VMEM_BYTES),
        cost_estimate=cost(6 * patches * width * slots, 4 * patches * width),
    )(shares, tokens, cotangent, dispatch, combine)


def token_kernel(dispatch_ref, inputs_ref, logit_ref, router_ref, grad_ref):
    grad = wide_dot(dispatch_ref[...].astype(LOW), inputs_ref[...], 1, 0)
    grad_ref[...] = (grad + wide_dot(logit_ref[...], router_ref[...], 1, 1)).astype(LOW)


def token_grads(dispatch, input_grads, logit_low, router):
    patches, slots = dispatch.shape
    width = router.shape[0]
    return pl.pallas_call(
        token_kernel,
        out_shape=jax.ShapeDtypeStruct((patches, width), LOW),
        in_specs=in_vmem(4),
        out_specs=in_vmem(1)[0],
        compiler_params=pltpu.CompilerParams(vmem_limit_bytes=VMEM_BYTES),
        cost_estimate=cost(4 * patches * width * slots, 4 * patches * width),
    )(dispatch, input_grads, logit_low, router)


def total_kernel(parts_ref, copies_ref):
    total = jnp.sum(parts_ref[...].astype(WIDE), axis=0).astype(copies_ref.dtype)
    copies_ref[...] = jnp.broadcast_to(total[None], copies_ref.shape)


def total_copies(parts, copies, kind):
    return pl.pallas_call(
        total_kernel,
        out_shape=jax.ShapeDtypeStruct((copies,) + parts.shape[1:], kind),
        in_specs=in_vmem(1),
        out_specs=in_vmem(1)[0],
        compiler_params=pltpu.CompilerParams(vmem_limit_bytes=VMEM_BYTES),
    )(parts)


def all_to_all(value, axes):
    return lax.all_to_all(value, axes, split_axis=0, concat_axis=0, tiled=True)


def sum_everywhere(term):
    near = lax.axis_size(NEAR)
    depth, width = term.shape
    parts = all_to_all(term.reshape(near, depth // near, width), NEAR)
    parts = all_to_all(total_copies(parts, lax.axis_size(REST), WIDE), REST)
    return all_to_all(total_copies(parts, near, LOW), NEAR).reshape(depth, width).astype(WIDE)


def host_moves():
    moves = []
    for slab in range(4):
        for yl in range(2):
            for core in range(2):
                place = 2 * slab + yl
                onward = (slab + core) % 2 == 0
                host = (place + (1 if onward else -1)) % 8
                moves.append((2 * place + core, 2 * host + (0 if onward else 1)))
    return moves


def move(value, moves):
    return lax.ppermute(value, COLUMN, moves)


def swap_cores(value):
    return lax.ppermute(value, "core", [(0, 1), (1, 0)])


def to_hosts(rows):
    return jnp.swapaxes(all_to_all(jnp.swapaxes(rows, 0, 1), HOSTS), 0, 1)


def shards(tokens, router, up_weight, down_weight, cotangent):
    tokens, cotangent = tokens[0], cotangent[0]
    moves = host_moves()
    up, down = move(up_weight[0], moves), move(down_weight[0], moves)

    dispatch, combine, sent = routing(tokens, router, cotangent)

    rows = lax.cond(lax.axis_index("x") < 4, to_hosts, lambda value: value, sent)
    rows, up, down = lax.optimization_barrier((rows, up, down))
    other = swap_cores(rows)
    other_share, other_act = expert_rows(other, up, down, LOW)
    got = swap_cores(other_share)
    share, act = expert_rows(rows, up, down, WIDE)
    back = to_hosts((share + got.astype(WIDE)).astype(LOW))
    input_grads, logit_low, term = logit_grads(back, tokens, cotangent, dispatch, combine)
    term, act = lax.optimization_barrier((term, act))
    grad_down = outer_sum(act, rows, other_act, other)
    grad_down = move(grad_down, [(there, here) for here, there in moves])
    grad_router = sum_everywhere(term)
    grad_tokens = token_grads(dispatch, input_grads, logit_low, router)
    return (grad_tokens[None], grad_router, grad_down[None])


def solution(mesh):
    sizes = (-1,) + tuple(EXPERT_SPLIT.values())
    images = P(EVERY, None, None)
    return jax.shard_map(
        shards,
        mesh=Mesh(mesh.devices.reshape(sizes), EVERY),
        in_specs=(images, P(), P(EXPERT, None, "dp"), P(EXPERT, "dp", None), images),
        out_specs=(images, P(), P(EXPERT, "dp", None)),
        check_vma=False,
    )
```

```python
import functools
import math

import jax
import jax.numpy as jnp
from jax import lax
from jax.experimental import pallas as pl
from jax.experimental.pallas import tpu as pltpu
from jax.sharding import Mesh
from jax.sharding import PartitionSpec as P

GELU_SCALE = math.sqrt(2.0 / math.pi)
GELU_CUBIC = 0.044715
LOW = jnp.bfloat16
WIDE = jnp.float32
EXPERT_SPLIT = {"yl": 2, "x": 4, "zh": 4, "zl": 2, "core": 2}
EXPERT = tuple(EXPERT_SPLIT)
EVERY = ("dp",) + EXPERT
NEAR = ("yl", "x", "zl", "core")
REST = ("dp", "zh")
COLUMN = ("dp", "yl", "core")
HOSTS = ("dp", "yl", "x", "zh", "zl")
VMEM_BYTES = 20 * 2**20


def wide_dot(left, right, left_dim, right_dim):
    return lax.dot_general(
        left, right, (((left_dim,), (right_dim,)), ((), ())), preferred_element_type=WIDE
    )


def in_vmem(count):
    return [pl.BlockSpec(memory_space=pltpu.VMEM)] * count


def in_hbm(count):
    return [pl.BlockSpec(memory_space=pltpu.HBM)] * count


def cost(flops, bytes_accessed):
    return pl.CostEstimate(flops=flops, bytes_accessed=bytes_accessed, transcendentals=0)


def host_block(slab, yl):
    return (1 - yl) * 2 + (slab + 1 - yl) % 2


def blocked(slots):
    rest = slots // 4
    slot = lax.broadcasted_iota(jnp.int32, (slots, slots), 0)
    place = lax.broadcasted_iota(jnp.int32, (slots, slots), 1)
    core = place // rest % 2
    here = (place // (2 * rest) * rest + place % rest) * 2 + core
    return jnp.where(slot == here, 1.0, 0.0).astype(LOW)


def routing_kernel(tokens_ref, router_ref, cotangent_ref, dispatch_ref, combine_ref, sent_ref):
    tokens = tokens_ref[...]
    slots = router_ref.shape[1]
    rest = slots // 4
    router = wide_dot(router_ref[...], blocked(slots), 1, 0).astype(LOW)
    logits = wide_dot(tokens, router, 1, 0)
    powers = jnp.exp(logits - jnp.max(logits, axis=0, keepdims=True))
    dispatch = powers / jnp.sum(powers, axis=0, keepdims=True)
    dispatch_ref[...] = dispatch
    inputs = wide_dot(dispatch.astype(LOW), tokens, 0, 0).astype(LOW)
    powers = jnp.exp(logits - jnp.max(logits, axis=1, keepdims=True))
    combine = powers / jnp.sum(powers, axis=1, keepdims=True)
    combine_ref[...] = combine
    grads = wide_dot(combine.astype(LOW), cotangent_ref[...], 0, 0).astype(LOW)
    for route, rows in enumerate((inputs, grads)):
        for chip in range(8):
            block = host_block(chip // 2, chip % 2) * rest
            sent_ref[route, chip * rest : (chip + 1) * rest] = rows[block : block + rest]


def routing(tokens, router, cotangent):
    patches, width = tokens.shape
    slots = router.shape[1]
    weights = jax.ShapeDtypeStruct((patches, slots), WIDE)
    return pl.pallas_call(
        routing_kernel,
        out_shape=(weights, weights, jax.ShapeDtypeStruct((2, 2 * slots, width), LOW)),
        in_specs=in_vmem(3),
        out_specs=tuple(in_vmem(3)),
        compiler_params=pltpu.CompilerParams(vmem_limit_bytes=VMEM_BYTES),
        cost_estimate=cost(6 * patches * width * slots, 4 * patches * width),
    )(tokens, router, cotangent)


def expert_kernel(rows_ref, up_ref, down_hbm, share_ref, act_ref, down_ref, sem):
    fetched = pltpu.make_async_copy(down_hbm, down_ref, sem)
    fetched.start()
    up = up_ref[...]
    hidden_pre = wide_dot(rows_ref[0], up, 1, 0)
    squared = hidden_pre * hidden_pre
    inner = jnp.tanh(GELU_SCALE * (hidden_pre + GELU_CUBIC * squared * hidden_pre))
    half = 0.5 * (1.0 + inner)
    activation = (hidden_pre * half).astype(LOW)
    act_ref[...] = activation
    fetched.wait()
    down = down_ref[...]
    share_ref[0] = wide_dot(activation, down, 1, 0).astype(share_ref.dtype)
    slope = half + 0.5 * hidden_pre * (1.0 - inner * inner) * (
        GELU_SCALE + 3.0 * GELU_SCALE * GELU_CUBIC * squared
    )
    upstream = wide_dot(rows_ref[1], down, 1, 1)
    hidden_grad = (upstream * slope).astype(LOW)
    share_ref[1] = wide_dot(hidden_grad, up, 1, 1).astype(share_ref.dtype)


def expert_rows(rows, up, down, kind):
    _, count, width = rows.shape
    hidden = up.shape[1]
    return pl.pallas_call(
        expert_kernel,
        out_shape=(
            jax.ShapeDtypeStruct(rows.shape, kind),
            jax.ShapeDtypeStruct((count, hidden), LOW),
        ),
        in_specs=in_vmem(2) + in_hbm(1),
        out_specs=tuple(in_vmem(2)),
        scratch_shapes=[pltpu.VMEM(down.shape, down.dtype), pltpu.SemaphoreType.DMA],
        compiler_params=pltpu.CompilerParams(vmem_limit_bytes=VMEM_BYTES),
        cost_estimate=cost(8 * count * width * hidden, 4 * width * hidden + 10 * count * width),
    )(rows, up, down)


def outer_kernel(act_ref, rows_ref, other_act_ref, other_rows_ref, grad_ref):
    total = wide_dot(act_ref[...], rows_ref[1], 0, 0)
    grad_ref[...] = (total + wide_dot(other_act_ref[...], other_rows_ref[1], 0, 0)).astype(LOW)


def outer_sum(act, rows, other_act, other_rows):
    count, hidden = act.shape
    width = rows.shape[2]
    return pl.pallas_call(
        outer_kernel,
        out_shape=jax.ShapeDtypeStruct((hidden, width), LOW),
        in_specs=in_vmem(4),
        out_specs=in_vmem(1)[0],
        compiler_params=pltpu.CompilerParams(vmem_limit_bytes=VMEM_BYTES),
        cost_estimate=cost(4 * count * width * hidden, 2 * hidden * width),
    )(act, rows, other_act, other_rows)


def settle_kernel(moved_ref, out_ref):
    out_ref[...] = moved_ref[...]


def settle(moved):
    return pl.pallas_call(
        settle_kernel,
        out_shape=jax.ShapeDtypeStruct(moved.shape, moved.dtype),
        in_specs=in_vmem(1),
        out_specs=in_vmem(1)[0],
        compiler_params=pltpu.CompilerParams(vmem_limit_bytes=VMEM_BYTES),
        cost_estimate=cost(0, 4 * moved.size),
    )(moved)


def logit_kernel(
    shares_ref, tokens_ref, cotangent_ref, dispatch_ref, combine_ref, inputs_ref, logit_ref, term_ref
):
    slots = dispatch_ref.shape[1]
    rest = slots // 4

    def total(route):
        parts = [None] * 4
        for chip in range(8):
            share = shares_ref[route, chip * rest : (chip + 1) * rest].astype(WIDE)
            block = host_block(chip // 2, chip % 2)
            parts[block] = share if parts[block] is None else parts[block] + share
        return jnp.concatenate([part.astype(LOW) for part in parts])

    tokens = tokens_ref[...]
    dispatch, combine = dispatch_ref[...], combine_ref[...]
    input_grads = total(1)
    inputs_ref[...] = input_grads
    grad = wide_dot(cotangent_ref[...], total(0), 1, 1)
    logit_grad = combine * (grad - jnp.sum(combine * grad, axis=1, keepdims=True))
    grad = wide_dot(tokens, input_grads, 1, 1)
    logit_grad = logit_grad + dispatch * (grad - jnp.sum(dispatch * grad, axis=0, keepdims=True))
    logit_low = wide_dot(logit_grad.astype(LOW), blocked(slots), 1, 1).astype(LOW)
    logit_ref[...] = logit_low
    term_ref[...] = wide_dot(tokens, logit_low, 0, 0).astype(LOW)


def logit_grads(shares, tokens, cotangent, dispatch, combine):
    patches, width = tokens.shape
    slots = dispatch.shape[1]
    return pl.pallas_call(
        logit_kernel,
        out_shape=(
            jax.ShapeDtypeStruct((slots, width), LOW),
            jax.ShapeDtypeStruct((patches, slots), LOW),
            jax.ShapeDtypeStruct((width, slots), LOW),
        ),
        in_specs=in_vmem(5),
        out_specs=tuple(in_vmem(3)),
        compiler_params=pltpu.CompilerParams(vmem_limit_bytes=VMEM_BYTES),
        cost_estimate=cost(6 * patches * width * slots, 4 * patches * width),
    )(shares, tokens, cotangent, dispatch, combine)


def token_kernel(dispatch_ref, inputs_ref, logit_ref, router_ref, grad_ref):
    grad = wide_dot(dispatch_ref[...].astype(LOW), inputs_ref[...], 1, 0)
    grad_ref[...] = (grad + wide_dot(logit_ref[...], router_ref[...], 1, 1)).astype(LOW)


def token_grads(dispatch, input_grads, logit_low, router):
    patches, slots = dispatch.shape
    width = router.shape[0]
    return pl.pallas_call(
        token_kernel,
        out_shape=jax.ShapeDtypeStruct((patches, width), LOW),
        in_specs=in_vmem(4),
        out_specs=in_vmem(1)[0],
        compiler_params=pltpu.CompilerParams(vmem_limit_bytes=VMEM_BYTES),
        cost_estimate=cost(4 * patches * width * slots, 4 * patches * width),
    )(dispatch, input_grads, logit_low, router)


def total_kernel(parts_ref, copies_ref):
    total = jnp.sum(parts_ref[...].astype(WIDE), axis=0).astype(copies_ref.dtype)
    copies_ref[...] = jnp.broadcast_to(total[None], copies_ref.shape)


def total_copies(parts, copies, kind):
    return pl.pallas_call(
        total_kernel,
        out_shape=jax.ShapeDtypeStruct((copies,) + parts.shape[1:], kind),
        in_specs=in_vmem(1),
        out_specs=in_vmem(1)[0],
        compiler_params=pltpu.CompilerParams(vmem_limit_bytes=VMEM_BYTES),
    )(parts)


def all_to_all(value, axes):
    return lax.all_to_all(value, axes, split_axis=0, concat_axis=0, tiled=True)


def sum_everywhere(term, beside):
    near = lax.axis_size(NEAR)
    depth, width = term.shape
    parts = all_to_all(term.reshape(near, depth // near, width), NEAR)
    parts = all_to_all(total_copies(parts, lax.axis_size(REST), WIDE), REST)
    copies, beside = lax.optimization_barrier((total_copies(parts, near, LOW), beside))
    return all_to_all(copies, NEAR).reshape(depth, width).astype(WIDE), beside


def host_moves():
    moves = []
    for slab in range(4):
        for yl in range(2):
            for core in range(2):
                place = 2 * slab + yl
                onward = (slab + core) % 2 == 0
                host = (place + (1 if onward else -1)) % 8
                moves.append((2 * place + core, 2 * host + (0 if onward else 1)))
    return moves


def move(value, moves):
    return lax.ppermute(value, COLUMN, moves)


def swap_cores(value):
    return lax.ppermute(value, "core", [(0, 1), (1, 0)])


def to_hosts(rows):
    return jnp.swapaxes(all_to_all(jnp.swapaxes(rows, 0, 1), HOSTS), 0, 1)


def shards(tokens, router, up_weight, down_weight, cotangent):
    tokens, cotangent = tokens[0], cotangent[0]
    moves = host_moves()
    up, down = move(up_weight[0], moves), move(down_weight[0], moves)

    dispatch, combine, sent = routing(tokens, router, cotangent)

    rows = lax.cond(lax.axis_index("x") < 4, to_hosts, lambda value: value, sent)
    rows, up, down = lax.optimization_barrier((rows, up, down))
    other = swap_cores(rows)
    other_share, other_act = expert_rows(other, up, down, LOW)
    got = swap_cores(other_share)
    share, act = expert_rows(rows, up, down, WIDE)
    back = to_hosts((share + got.astype(WIDE)).astype(LOW))
    input_grads, logit_low, term = logit_grads(back, tokens, cotangent, dispatch, combine)
    term, act = lax.optimization_barrier((term, act))
    grad_down = outer_sum(act, rows, other_act, other)
    grad_down = move(grad_down, [(there, here) for here, there in moves])
    grad_router, grad_down = sum_everywhere(term, grad_down)
    grad_tokens = token_grads(dispatch, input_grads, logit_low, router)
    return (grad_tokens[None], grad_router, settle(grad_down)[None])


def solution(mesh):
    sizes = (-1,) + tuple(EXPERT_SPLIT.values())
    images = P(EVERY, None, None)
    return jax.shard_map(
        shards,
        mesh=Mesh(mesh.devices.reshape(sizes), EVERY),
        in_specs=(images, P(), P(EXPERT, None, "dp"), P(EXPERT, "dp", None), images),
        out_specs=(images, P(), P(EXPERT, "dp", None)),
        check_vma=False,
    )
```

```python
import functools
import math

import jax
import jax.numpy as jnp
from jax import lax
from jax.experimental import pallas as pl
from jax.experimental.pallas import tpu as pltpu
from jax.sharding import Mesh
from jax.sharding import PartitionSpec as P

GELU_SCALE = math.sqrt(2.0 / math.pi)
GELU_CUBIC = 0.044715
LOW = jnp.bfloat16
WIDE = jnp.float32
EXPERT_SPLIT = {"yl": 2, "x": 4, "zh": 4, "zl": 2, "core": 2}
EXPERT = tuple(EXPERT_SPLIT)
EVERY = ("dp",) + EXPERT
NEAR = ("yl", "x", "zl", "core")
REST = ("dp", "zh")
COLUMN = ("dp", "yl", "core")
HOSTS = ("dp", "yl", "x", "zh", "zl")
VMEM_BYTES = 20 * 2**20


def wide_dot(left, right, left_dim, right_dim):
    return lax.dot_general(
        left, right, (((left_dim,), (right_dim,)), ((), ())), preferred_element_type=WIDE
    )


def in_vmem(count):
    return [pl.BlockSpec(memory_space=pltpu.VMEM)] * count


def in_hbm(count):
    return [pl.BlockSpec(memory_space=pltpu.HBM)] * count


def cost(flops, bytes_accessed):
    return pl.CostEstimate(flops=flops, bytes_accessed=bytes_accessed, transcendentals=0)


def host_block(slab, yl):
    return (1 - yl) * 2 + (slab + 1 - yl) % 2


def blocked(slots):
    rest = slots // 4
    slot = lax.broadcasted_iota(jnp.int32, (slots, slots), 0)
    place = lax.broadcasted_iota(jnp.int32, (slots, slots), 1)
    core = place // rest % 2
    here = (place // (2 * rest) * rest + place % rest) * 2 + core
    return jnp.where(slot == here, 1.0, 0.0).astype(LOW)


def routing_kernel(tokens_ref, router_ref, cotangent_ref, dispatch_ref, combine_ref, sent_ref):
    tokens = tokens_ref[...]
    slots = router_ref.shape[1]
    rest = slots // 4
    router = wide_dot(router_ref[...], blocked(slots), 1, 0).astype(LOW)
    logits = wide_dot(tokens, router, 1, 0)
    powers = jnp.exp(logits - jnp.max(logits, axis=0, keepdims=True))
    dispatch = powers / jnp.sum(powers, axis=0, keepdims=True)
    dispatch_ref[...] = dispatch
    inputs = wide_dot(dispatch.astype(LOW), tokens, 0, 0).astype(LOW)
    powers = jnp.exp(logits - jnp.max(logits, axis=1, keepdims=True))
    combine = powers / jnp.sum(powers, axis=1, keepdims=True)
    combine_ref[...] = combine
    grads = wide_dot(combine.astype(LOW), cotangent_ref[...], 0, 0).astype(LOW)
    for route, rows in enumerate((inputs, grads)):
        for chip in range(8):
            block = host_block(chip // 2, chip % 2) * rest
            sent_ref[route, chip * rest : (chip + 1) * rest] = rows[block : block + rest]


def routing(tokens, router, cotangent):
    patches, width = tokens.shape
    slots = router.shape[1]
    weights = jax.ShapeDtypeStruct((patches, slots), WIDE)
    return pl.pallas_call(
        routing_kernel,
        out_shape=(weights, weights, jax.ShapeDtypeStruct((2, 2 * slots, width), LOW)),
        in_specs=in_vmem(3),
        out_specs=tuple(in_vmem(3)),
        compiler_params=pltpu.CompilerParams(vmem_limit_bytes=VMEM_BYTES),
        cost_estimate=cost(6 * patches * width * slots, 4 * patches * width),
    )(tokens, router, cotangent)


def expert_kernel(rows_ref, up_ref, down_hbm, share_ref, act_ref, down_ref, sem):
    fetched = pltpu.make_async_copy(down_hbm, down_ref, sem)
    fetched.start()
    up = up_ref[...]
    hidden_pre = wide_dot(rows_ref[0], up, 1, 0)
    squared = hidden_pre * hidden_pre
    inner = jnp.tanh(GELU_SCALE * (hidden_pre + GELU_CUBIC * squared * hidden_pre))
    half = 0.5 * (1.0 + inner)
    activation = (hidden_pre * half).astype(LOW)
    act_ref[...] = activation
    fetched.wait()
    down = down_ref[...]
    share_ref[0] = wide_dot(activation, down, 1, 0).astype(share_ref.dtype)
    slope = half + 0.5 * hidden_pre * (1.0 - inner * inner) * (
        GELU_SCALE + 3.0 * GELU_SCALE * GELU_CUBIC * squared
    )
    upstream = wide_dot(rows_ref[1], down, 1, 1)
    hidden_grad = (upstream * slope).astype(LOW)
    share_ref[1] = wide_dot(hidden_grad, up, 1, 1).astype(share_ref.dtype)


def expert_rows(rows, up, down, kind):
    _, count, width = rows.shape
    hidden = up.shape[1]
    return pl.pallas_call(
        expert_kernel,
        out_shape=(
            jax.ShapeDtypeStruct(rows.shape, kind),
            jax.ShapeDtypeStruct((count, hidden), LOW),
        ),
        in_specs=in_vmem(2) + in_hbm(1),
        out_specs=tuple(in_vmem(2)),
        scratch_shapes=[pltpu.VMEM(down.shape, down.dtype), pltpu.SemaphoreType.DMA],
        compiler_params=pltpu.CompilerParams(vmem_limit_bytes=VMEM_BYTES),
        cost_estimate=cost(8 * count * width * hidden, 4 * width * hidden + 10 * count * width),
    )(rows, up, down)


def outer_kernel(act_ref, rows_ref, other_act_ref, other_rows_ref, grad_ref):
    total = wide_dot(act_ref[...], rows_ref[1], 0, 0)
    grad_ref[...] = (total + wide_dot(other_act_ref[...], other_rows_ref[1], 0, 0)).astype(LOW)


def outer_sum(act, rows, other_act, other_rows):
    count, hidden = act.shape
    width = rows.shape[2]
    return pl.pallas_call(
        outer_kernel,
        out_shape=jax.ShapeDtypeStruct((hidden, width), LOW),
        in_specs=in_vmem(4),
        out_specs=in_vmem(1)[0],
        compiler_params=pltpu.CompilerParams(vmem_limit_bytes=VMEM_BYTES),
        cost_estimate=cost(4 * count * width * hidden, 2 * hidden * width),
    )(act, rows, other_act, other_rows)


def settle_kernel(moved_ref, out_ref):
    out_ref[...] = moved_ref[...]


def settle(moved):
    return pl.pallas_call(
        settle_kernel,
        out_shape=jax.ShapeDtypeStruct(moved.shape, moved.dtype),
        in_specs=in_vmem(1),
        out_specs=in_vmem(1)[0],
        compiler_params=pltpu.CompilerParams(vmem_limit_bytes=VMEM_BYTES),
        cost_estimate=cost(0, 4 * moved.size),
    )(moved)


def logit_kernel(
    shares_ref, tokens_ref, cotangent_ref, dispatch_ref, combine_ref, inputs_ref, logit_ref, term_ref
):
    slots = dispatch_ref.shape[1]
    rest = slots // 4

    def total(route):
        parts = [None] * 4
        for chip in range(8):
            share = shares_ref[route, chip * rest : (chip + 1) * rest].astype(WIDE)
            block = host_block(chip // 2, chip % 2)
            parts[block] = share if parts[block] is None else parts[block] + share
        return jnp.concatenate([part.astype(LOW) for part in parts])

    tokens = tokens_ref[...]
    dispatch, combine = dispatch_ref[...], combine_ref[...]
    input_grads = total(1)
    inputs_ref[...] = input_grads
    grad = wide_dot(cotangent_ref[...], total(0), 1, 1)
    logit_grad = combine * (grad - jnp.sum(combine * grad, axis=1, keepdims=True))
    grad = wide_dot(tokens, input_grads, 1, 1)
    logit_grad = logit_grad + dispatch * (grad - jnp.sum(dispatch * grad, axis=0, keepdims=True))
    logit_low = wide_dot(logit_grad.astype(LOW), blocked(slots), 1, 1).astype(LOW)
    logit_ref[...] = logit_low
    term_ref[...] = wide_dot(tokens, logit_low, 0, 0).astype(LOW)


def logit_grads(shares, tokens, cotangent, dispatch, combine):
    patches, width = tokens.shape
    slots = dispatch.shape[1]
    return pl.pallas_call(
        logit_kernel,
        out_shape=(
            jax.ShapeDtypeStruct((slots, width), LOW),
            jax.ShapeDtypeStruct((patches, slots), LOW),
            jax.ShapeDtypeStruct((width, slots), LOW),
        ),
        in_specs=in_vmem(5),
        out_specs=tuple(in_vmem(3)),
        compiler_params=pltpu.CompilerParams(vmem_limit_bytes=VMEM_BYTES),
        cost_estimate=cost(6 * patches * width * slots, 4 * patches * width),
    )(shares, tokens, cotangent, dispatch, combine)


def token_kernel(dispatch_ref, inputs_ref, logit_ref, router_ref, grad_ref):
    grad = wide_dot(dispatch_ref[...].astype(LOW), inputs_ref[...], 1, 0)
    grad_ref[...] = (grad + wide_dot(logit_ref[...], router_ref[...], 1, 1)).astype(LOW)


def token_grads(dispatch, input_grads, logit_low, router):
    patches, slots = dispatch.shape
    width = router.shape[0]
    return pl.pallas_call(
        token_kernel,
        out_shape=jax.ShapeDtypeStruct((patches, width), LOW),
        in_specs=in_vmem(4),
        out_specs=in_vmem(1)[0],
        compiler_params=pltpu.CompilerParams(vmem_limit_bytes=VMEM_BYTES),
        cost_estimate=cost(4 * patches * width * slots, 4 * patches * width),
    )(dispatch, input_grads, logit_low, router)


def total_kernel(parts_ref, copies_ref):
    total = jnp.sum(parts_ref[...].astype(WIDE), axis=0).astype(copies_ref.dtype)
    copies_ref[...] = jnp.broadcast_to(total[None], copies_ref.shape)


def total_copies(parts, copies, kind):
    return pl.pallas_call(
        total_kernel,
        out_shape=jax.ShapeDtypeStruct((copies,) + parts.shape[1:], kind),
        in_specs=in_vmem(1),
        out_specs=in_vmem(1)[0],
        compiler_params=pltpu.CompilerParams(vmem_limit_bytes=VMEM_BYTES),
    )(parts)


def all_to_all(value, axes):
    return lax.all_to_all(value, axes, split_axis=0, concat_axis=0, tiled=True)


def sum_everywhere(term):
    near = lax.axis_size(NEAR)
    depth, width = term.shape
    parts = all_to_all(term.reshape(near, depth // near, width), NEAR)
    parts = all_to_all(total_copies(parts, lax.axis_size(REST), WIDE), REST)
    return all_to_all(total_copies(parts, near, LOW), NEAR).reshape(depth, width).astype(WIDE)


def host_moves():
    moves = []
    for slab in range(4):
        for yl in range(2):
            for core in range(2):
                place = 2 * slab + yl
                onward = (slab + core) % 2 == 0
                host = (place + (1 if onward else -1)) % 8
                moves.append((2 * place + core, 2 * host + (0 if onward else 1)))
    return moves


def move(value, moves):
    return lax.ppermute(value, COLUMN, moves)


def swap_cores(value):
    return lax.ppermute(value, "core", [(0, 1), (1, 0)])


def to_hosts(rows):
    return jnp.swapaxes(all_to_all(jnp.swapaxes(rows, 0, 1), HOSTS), 0, 1)


def shards(tokens, router, up_weight, down_weight, cotangent):
    tokens, cotangent = tokens[0], cotangent[0]
    moves = host_moves()
    up, down = move(up_weight[0], moves), move(down_weight[0], moves)

    dispatch, combine, sent = routing(tokens, router, cotangent)

    rows = lax.cond(lax.axis_index("x") < 4, to_hosts, lambda value: value, sent)
    rows, up, down = lax.optimization_barrier((rows, up, down))
    other = swap_cores(rows)
    other_share, other_act = expert_rows(other, up, down, LOW)
    got = swap_cores(other_share)
    share, act = expert_rows(rows, up, down, WIDE)
    back = to_hosts((share + got.astype(WIDE)).astype(LOW))
    input_grads, logit_low, term = logit_grads(back, tokens, cotangent, dispatch, combine)
    term, act = lax.optimization_barrier((term, act))
    grad_down = outer_sum(act, rows, other_act, other)
    grad_down = move(grad_down, [(there, here) for here, there in moves])
    grad_router = sum_everywhere(term)
    grad_tokens = token_grads(dispatch, input_grads, logit_low, router)
    return (grad_tokens[None], grad_router, settle(grad_down)[None])


def solution(mesh):
    sizes = (-1,) + tuple(EXPERT_SPLIT.values())
    images = P(EVERY, None, None)
    return jax.shard_map(
        shards,
        mesh=Mesh(mesh.devices.reshape(sizes), EVERY),
        in_specs=(images, P(), P(EXPERT, None, "dp"), P(EXPERT, "dp", None), images),
        out_specs=(images, P(), P(EXPERT, "dp", None)),
        check_vma=False,
    )
```

```python
import functools
import math

import jax
import jax.numpy as jnp
from jax import lax
from jax.experimental import pallas as pl
from jax.experimental.pallas import tpu as pltpu
from jax.sharding import Mesh
from jax.sharding import PartitionSpec as P

GELU_SCALE = math.sqrt(2.0 / math.pi)
GELU_CUBIC = 0.044715
LOW = jnp.bfloat16
WIDE = jnp.float32
EXPERT_SPLIT = {"yl": 2, "x": 4, "zh": 4, "zl": 2, "core": 2}
EXPERT = tuple(EXPERT_SPLIT)
EVERY = ("dp",) + EXPERT
NEAR = ("yl", "x", "zl", "core")
REST = ("dp", "zh")
COLUMN = ("dp", "yl", "core")
HOSTS = ("dp", "yl", "x", "zh", "zl")
VMEM_BYTES = 20 * 2**20


def wide_dot(left, right, left_dim, right_dim):
    return lax.dot_general(
        left, right, (((left_dim,), (right_dim,)), ((), ())), preferred_element_type=WIDE
    )


def in_vmem(count):
    return [pl.BlockSpec(memory_space=pltpu.VMEM)] * count


def in_hbm(count):
    return [pl.BlockSpec(memory_space=pltpu.HBM)] * count


def cost(flops, bytes_accessed):
    return pl.CostEstimate(flops=flops, bytes_accessed=bytes_accessed, transcendentals=0)


def host_block(slab, yl):
    return (1 - yl) * 2 + (slab + 1 - yl) % 2


def blocked(slots):
    rest = slots // 4
    slot = lax.broadcasted_iota(jnp.int32, (slots, slots), 0)
    place = lax.broadcasted_iota(jnp.int32, (slots, slots), 1)
    core = place // rest % 2
    here = (place // (2 * rest) * rest + place % rest) * 2 + core
    return jnp.where(slot == here, 1.0, 0.0).astype(LOW)


def routing_kernel(tokens_ref, router_ref, cotangent_ref, dispatch_ref, combine_ref, sent_ref):
    tokens = tokens_ref[...]
    slots = router_ref.shape[1]
    rest = slots // 4
    router = wide_dot(router_ref[...], blocked(slots), 1, 0).astype(LOW)
    logits = wide_dot(tokens, router, 1, 0)
    powers = jnp.exp(logits - jnp.max(logits, axis=0, keepdims=True))
    dispatch = powers / jnp.sum(powers, axis=0, keepdims=True)
    dispatch_ref[...] = dispatch
    inputs = wide_dot(dispatch.astype(LOW), tokens, 0, 0).astype(LOW)
    powers = jnp.exp(logits - jnp.max(logits, axis=1, keepdims=True))
    combine = powers / jnp.sum(powers, axis=1, keepdims=True)
    combine_ref[...] = combine
    grads = wide_dot(combine.astype(LOW), cotangent_ref[...], 0, 0).astype(LOW)
    for route, rows in enumerate((inputs, grads)):
        for chip in range(8):
            block = host_block(chip // 2, chip % 2) * rest
            sent_ref[route, chip * rest : (chip + 1) * rest] = rows[block : block + rest]


def routing(tokens, router, cotangent):
    patches, width = tokens.shape
    slots = router.shape[1]
    weights = jax.ShapeDtypeStruct((patches, slots), WIDE)
    return pl.pallas_call(
        routing_kernel,
        out_shape=(weights, weights, jax.ShapeDtypeStruct((2, 2 * slots, width), LOW)),
        in_specs=in_vmem(3),
        out_specs=tuple(in_vmem(3)),
        compiler_params=pltpu.CompilerParams(vmem_limit_bytes=VMEM_BYTES),
        cost_estimate=cost(6 * patches * width * slots, 4 * patches * width),
    )(tokens, router, cotangent)


def expert_kernel(rows_ref, up_ref, down_hbm, share_ref, act_ref, down_ref, sem):
    fetched = pltpu.make_async_copy(down_hbm, down_ref, sem)
    fetched.start()
    up = up_ref[...]
    hidden_pre = wide_dot(rows_ref[0], up, 1, 0)
    squared = hidden_pre * hidden_pre
    inner = jnp.tanh(GELU_SCALE * (hidden_pre + GELU_CUBIC * squared * hidden_pre))
    half = 0.5 * (1.0 + inner)
    activation = (hidden_pre * half).astype(LOW)
    act_ref[...] = activation
    fetched.wait()
    down = down_ref[...]
    share_ref[0] = wide_dot(activation, down, 1, 0).astype(share_ref.dtype)
    slope = half + 0.5 * hidden_pre * (1.0 - inner * inner) * (
        GELU_SCALE + 3.0 * GELU_SCALE * GELU_CUBIC * squared
    )
    upstream = wide_dot(rows_ref[1], down, 1, 1)
    hidden_grad = (upstream * slope).astype(LOW)
    share_ref[1] = wide_dot(hidden_grad, up, 1, 1).astype(share_ref.dtype)


def expert_rows(rows, up, down, kind):
    _, count, width = rows.shape
    hidden = up.shape[1]
    return pl.pallas_call(
        expert_kernel,
        out_shape=(
            jax.ShapeDtypeStruct(rows.shape, kind),
            jax.ShapeDtypeStruct((count, hidden), LOW),
        ),
        in_specs=in_vmem(2) + in_hbm(1),
        out_specs=tuple(in_vmem(2)),
        scratch_shapes=[pltpu.VMEM(down.shape, down.dtype), pltpu.SemaphoreType.DMA],
        compiler_params=pltpu.CompilerParams(vmem_limit_bytes=VMEM_BYTES),
        cost_estimate=cost(8 * count * width * hidden, 4 * width * hidden + 10 * count * width),
    )(rows, up, down)


def outer_kernel(act_ref, rows_ref, other_act_ref, other_rows_ref, grad_ref):
    total = wide_dot(act_ref[...], rows_ref[1], 0, 0)
    grad_ref[...] = (total + wide_dot(other_act_ref[...], other_rows_ref[1], 0, 0)).astype(LOW)


def outer_sum(act, rows, other_act, other_rows):
    count, hidden = act.shape
    width = rows.shape[2]
    return pl.pallas_call(
        outer_kernel,
        out_shape=jax.ShapeDtypeStruct((hidden, width), LOW),
        in_specs=in_vmem(4),
        out_specs=in_vmem(1)[0],
        compiler_params=pltpu.CompilerParams(vmem_limit_bytes=VMEM_BYTES),
        cost_estimate=cost(4 * count * width * hidden, 2 * hidden * width),
    )(act, rows, other_act, other_rows)


def logit_kernel(
    shares_ref, tokens_ref, cotangent_ref, dispatch_ref, combine_ref, inputs_ref, logit_ref, term_ref
):
    slots = dispatch_ref.shape[1]
    rest = slots // 4

    def total(route):
        parts = [None] * 4
        for chip in range(8):
            share = shares_ref[route, chip * rest : (chip + 1) * rest].astype(WIDE)
            block = host_block(chip // 2, chip % 2)
            parts[block] = share if parts[block] is None else parts[block] + share
        return jnp.concatenate([part.astype(LOW) for part in parts])

    tokens = tokens_ref[...]
    dispatch, combine = dispatch_ref[...], combine_ref[...]
    input_grads = total(1)
    inputs_ref[...] = input_grads
    grad = wide_dot(cotangent_ref[...], total(0), 1, 1)
    logit_grad = combine * (grad - jnp.sum(combine * grad, axis=1, keepdims=True))
    grad = wide_dot(tokens, input_grads, 1, 1)
    logit_grad = logit_grad + dispatch * (grad - jnp.sum(dispatch * grad, axis=0, keepdims=True))
    logit_low = wide_dot(logit_grad.astype(LOW), blocked(slots), 1, 1).astype(LOW)
    logit_ref[...] = logit_low
    term_ref[...] = wide_dot(tokens, logit_low, 0, 0).astype(LOW)


def logit_grads(shares, tokens, cotangent, dispatch, combine):
    patches, width = tokens.shape
    slots = dispatch.shape[1]
    return pl.pallas_call(
        logit_kernel,
        out_shape=(
            jax.ShapeDtypeStruct((slots, width), LOW),
            jax.ShapeDtypeStruct((patches, slots), LOW),
            jax.ShapeDtypeStruct((width, slots), LOW),
        ),
        in_specs=in_vmem(5),
        out_specs=tuple(in_vmem(3)),
        compiler_params=pltpu.CompilerParams(vmem_limit_bytes=VMEM_BYTES),
        cost_estimate=cost(6 * patches * width * slots, 4 * patches * width),
    )(shares, tokens, cotangent, dispatch, combine)


def token_kernel(dispatch_ref, inputs_ref, logit_ref, router_ref, grad_ref):
    grad = wide_dot(dispatch_ref[...].astype(LOW), inputs_ref[...], 1, 0)
    grad_ref[...] = (grad + wide_dot(logit_ref[...], router_ref[...], 1, 1)).astype(LOW)


def token_grads(dispatch, input_grads, logit_low, router):
    patches, slots = dispatch.shape
    width = router.shape[0]
    return pl.pallas_call(
        token_kernel,
        out_shape=jax.ShapeDtypeStruct((patches, width), LOW),
        in_specs=in_vmem(4),
        out_specs=in_vmem(1)[0],
        compiler_params=pltpu.CompilerParams(vmem_limit_bytes=VMEM_BYTES),
        cost_estimate=cost(4 * patches * width * slots, 4 * patches * width),
    )(dispatch, input_grads, logit_low, router)


def total_kernel(parts_ref, copies_ref):
    total = jnp.sum(parts_ref[...].astype(WIDE), axis=0).astype(copies_ref.dtype)
    copies_ref[...] = jnp.broadcast_to(total[None], copies_ref.shape)


def total_copies(parts, copies, kind):
    return pl.pallas_call(
        total_kernel,
        out_shape=jax.ShapeDtypeStruct((copies,) + parts.shape[1:], kind),
        in_specs=in_vmem(1),
        out_specs=in_vmem(1)[0],
        compiler_params=pltpu.CompilerParams(vmem_limit_bytes=VMEM_BYTES),
    )(parts)


def all_to_all(value, axes):
    return lax.all_to_all(value, axes, split_axis=0, concat_axis=0, tiled=True)


def sum_everywhere(term):
    near = lax.axis_size(NEAR)
    depth, width = term.shape
    parts = all_to_all(term.reshape(near, depth // near, width), NEAR)
    parts = all_to_all(total_copies(parts, lax.axis_size(REST), WIDE), REST)
    return all_to_all(total_copies(parts, near, LOW), NEAR).reshape(depth, width).astype(WIDE)


def host_moves():
    moves = []
    for slab in range(4):
        for yl in range(2):
            for core in range(2):
                place = 2 * slab + yl
                onward = (slab + core) % 2 == 0
                host = (place + (1 if onward else -1)) % 8
                moves.append((2 * place + core, 2 * host + (0 if onward else 1)))
    return moves


def move(value, moves):
    return lax.ppermute(value, COLUMN, moves)


def swap_cores(value):
    return lax.ppermute(value, "core", [(0, 1), (1, 0)])


def to_hosts(rows):
    return jnp.swapaxes(all_to_all(jnp.swapaxes(rows, 0, 1), HOSTS), 0, 1)


def shards(tokens, router, up_weight, down_weight, cotangent):
    tokens, cotangent = tokens[0], cotangent[0]
    moves = host_moves()
    up, down = move(up_weight[0], moves), move(down_weight[0], moves)

    dispatch, combine, sent = routing(tokens, router, cotangent)

    rows = lax.cond(lax.axis_index("x") < 4, to_hosts, lambda value: value, sent)
    rows, up, down = lax.optimization_barrier((rows, up, down))
    other = swap_cores(rows)
    other_share, other_act = expert_rows(other, up, down, LOW)
    got = swap_cores(other_share)
    share, act = expert_rows(rows, up, down, WIDE)
    back = to_hosts((share + got.astype(WIDE)).astype(LOW))
    input_grads, logit_low, term = logit_grads(back, tokens, cotangent, dispatch, combine)
    term, act = lax.optimization_barrier((term, act))
    grad_down = outer_sum(act, rows, other_act, other)
    grad_down = move(grad_down, [(there, here) for here, there in moves])
    grad_router = sum_everywhere(term)
    grad_tokens = token_grads(dispatch, input_grads, logit_low, router)
    return (grad_tokens[None], grad_router, grad_down[None])


def solution(mesh):
    sizes = (-1,) + tuple(EXPERT_SPLIT.values())
    images = P(EVERY, None, None)
    return jax.shard_map(
        shards,
        mesh=Mesh(mesh.devices.reshape(sizes), EVERY),
        in_specs=(images, P(), P(EXPERT, None, "dp"), P(EXPERT, "dp", None), images),
        out_specs=(images, P(), P(EXPERT, "dp", None)),
        check_vma=False,
    )
```
